32 devices in a mesh: az: 8 (over z, x), ch: 4 (over y, core).
Axes of the slice: x: 2, y: 2, z: 4, core: 2. Of those that a mesh axis runs over, the one named last changes fastest.
Arguments:
- features: bfloat16 [256, 32, 256], P(None, 'az'), may hold values from -6 to 6
- conv1_weight: bfloat16 [256, 3, 3, 256], P('ch'), may hold values from -0.125 to 0.125
- conv1_bias: float32 [256], P('ch'), may hold values from -3 to 3
- conv2_weight: bfloat16 [256, 3, 3, 256], P('ch'), may hold values from -0.125 to 0.125
- conv2_bias: float32 [256], P('ch'), may hold values from -3 to 3
- request_cell: int32 [32768], P('az'), may hold values from 0 to 1023, as said below
- corner_slot: int32 [4, 4096], P(None, 'az'), may hold values from 0 to 4095, as said below
- corner_frac: float32 [2, 4096], P(None, 'az'), may hold values from 0 to 1
- expand_weight: bfloat16 [256, 512], P('ch'), may hold values from -0.375 to 0.375
- expand_bias: float32 [512], P('ch'), may hold values from -3 to 3
Outputs:
- occupancy: bfloat16 [512, 4096], P('ch', 'az')
The draws below stay inside these ranges and needn't reach their ends.
Inputs may be any that keep to these rules, and one draw needn't show every extreme that they name: `request_cell`: cell index a * 256 + r within the sector that the slot's block names; entries of slots that no corner_slot entry names are never read. `corner_slot`: within one tile the 2048 entries name distinct slots; at most 512 slots of one sector block are named, exactly 512 for some sector of every tile.
All inputs are finite; a program needn't handle non-finite values.
Results may differ from the reference program's by a relative error of at most 0.014.
Values may be sent and summed in bfloat16 or wider, within the bound.
No kernel may reach another device: no remote copies, remote signals or barrier semaphores. Data moves between devices by JAX's collectives and lax.ppermute only.
A program may use at most 64 MiB of HBM per device.

```python
import jax
import jax.numpy as jnp
from jax import lax

C = 256
R = 256
CART_DEV = 512
A = 32
CELLS_DEV = 1024
CART = 4096
MEAN_REQ = 256
CAP = 512
HH = 512
N_AZ = 8
N_CH = 4


def tile_perm(subkey):
    return jax.random.permutation(subkey, 4 * CART_DEV)


def slot_table(key):
    base = jax.random.fold_in(key, 11)
    key_one, key_two, key_three, key_four = jax.random.split(base, 4)
    half = N_AZ // 2
    spread = jax.random.randint(key_one, (N_AZ, half), 0, MEAN_REQ + 1)
    chosen = jax.random.randint(key_two, (N_AZ,), 0, half)
    chosen = chosen.at[0].set(half - 1)
    sign_flip = jax.random.randint(key_three, (N_AZ, half), 0, 2) * 2 - 1
    sign_flip = sign_flip.at[0, half - 1].set(-1)
    marks = jnp.arange(half)[None, :] == chosen[:, None]
    spread = jnp.where(marks, MEAN_REQ, spread)
    counts = jnp.concatenate([MEAN_REQ + sign_flip * spread, MEAN_REQ - sign_flip * spread], axis=1)
    position = jnp.arange(CAP)
    used = (position[None, None, :] < counts[:, :, None]).reshape(N_AZ, N_AZ * CAP)
    order = jnp.argsort(1 - used.astype(jnp.int32), axis=1, stable=True)[:, :4 * CART_DEV]
    perms = jax.vmap(tile_perm)(jax.random.split(key_four, N_AZ))
    slots = jnp.take_along_axis(order, perms, axis=1)
    return slots.reshape(N_AZ, 4, CART_DEV).transpose(1, 0, 2).reshape(4, N_AZ * CART_DEV).astype(jnp.int32)


def draw_corner_slot(key, part):
    return slot_table(key)


def draw_request_cell(key, part):
    subkey = jax.random.fold_in(key, 23)
    cells = jax.random.randint(subkey, (N_AZ * N_AZ * CAP,), 0, CELLS_DEV)
    cells = cells.at[0].set(CELLS_DEV - 1)
    return cells.astype(jnp.int32)


def steps_of(stream_key, dims, cuts, least, top_value):
    def one(dim, shards_of):
        draws = jax.random.uniform(jax.random.fold_in(jax.random.fold_in(stream_key, 6), dim), (shards_of,), jnp.float32, least / len(cuts), top_value / len(cuts))
        return jnp.repeat(jnp.exp(draws), dims[dim] // shards_of).reshape((-1,) + (1,) * (len(dims) - dim - 1))

    level = one(*cuts[0])
    for cut in cuts[1:]:
        level = level * one(*cut)
    return level


def noise(stream_key, shape, scale, most, pieces=(), dtype=jnp.bfloat16):
    result = scale * jax.random.normal(stream_key, shape, jnp.float32)
    if pieces:
        result = result * steps_of(stream_key, shape, pieces, -0.22, 0.18)
    return jnp.clip(result, -most, most).astype(dtype)


def setup_inputs(seed: int = 0) -> dict:
    keys = jax.random.split(jax.random.key(seed), 11)
    features = noise(keys[0], (C, A, R), 1.0, 6.0, ((1, 8),))
    conv1_weight = noise(keys[1], (C, 3, 3, C), (9 * C) ** -0.5, 0.125, ((0, 4),))
    conv1_bias = noise(keys[2], (C,), 0.5, 3.0, ((0, 4),), jnp.float32)
    conv2_weight = noise(keys[3], (C, 3, 3, C), (9 * C) ** -0.5, 0.125, ((0, 4),))
    conv2_bias = noise(keys[4], (C,), 0.5, 3.0, ((0, 4),), jnp.float32)
    request_cell = draw_request_cell(jax.random.fold_in(keys[10], 71), 0)
    corner_slot = draw_corner_slot(jax.random.fold_in(keys[10], 71), 0)
    corner_frac = jnp.clip(1.0 * jax.random.uniform(keys[7], (2, CART), jnp.float32) ** steps_of(keys[7], (2, CART), ((1, 8),), -0.2, 0.2), 0.0, 1.0)
    expand_weight = noise(keys[8], (C, HH), C ** -0.5, 0.375, ((0, 4),))
    expand_bias = noise(keys[9], (HH,), 0.5, 3.0, ((0, 4),), jnp.float32)
    return dict(features=features, conv1_weight=conv1_weight, conv1_bias=conv1_bias, conv2_weight=conv2_weight, conv2_bias=conv2_bias, request_cell=request_cell, corner_slot=corner_slot, corner_frac=corner_frac, expand_weight=expand_weight, expand_bias=expand_bias)


def convolve(padded, weight, columns, ranges):
    inputs = padded.shape[0]
    ranged = jnp.pad(padded, ((0, 0), (0, 0), (1, 1)))
    running = jnp.zeros((weight.shape[0], columns * ranges), jnp.float32)
    for tap_az in range(3):
        for tap_rg in range(3):
            window = ranged[:, tap_az:tap_az + columns, tap_rg:tap_rg + ranges].reshape(inputs, columns * ranges)
            running = running + jnp.dot(weight[:, tap_az, tap_rg, :], window, preferred_element_type=jnp.float32)
    return running


def wrap_pad(field):
    return jnp.concatenate([field[:, -1:], field, field[:, :1]], axis=1)


def reference(features, conv1_weight, conv1_bias, conv2_weight, conv2_bias, request_cell, corner_slot, corner_frac, expand_weight, expand_bias):
    azimuths = features.shape[1]
    ranges = features.shape[2]
    hidden_one = jax.nn.relu(convolve(wrap_pad(features), conv1_weight, azimuths, ranges) + conv1_bias[:, None]).astype(jnp.bfloat16)
    hidden_one = hidden_one.reshape(-1, azimuths, ranges)
    hidden_two = jax.nn.relu(convolve(wrap_pad(hidden_one), conv2_weight, azimuths, ranges) + conv2_bias[:, None]).astype(jnp.bfloat16)
    table = request_cell.reshape(N_AZ, N_AZ * CAP)
    slots = corner_slot.reshape(4, N_AZ, CART_DEV)
    local_cells = jnp.take_along_axis(jnp.broadcast_to(table[None], (4,) + table.shape), slots, axis=2)
    global_cells = ((slots // CAP) * CELLS_DEV + local_cells).reshape(4, N_AZ * CART_DEV).astype(jnp.int32)
    frac_range = corner_frac[0][None, :]
    frac_azim = corner_frac[1][None, :]
    weights = [(1.0 - frac_range) * (1.0 - frac_azim), frac_range * (1.0 - frac_azim), (1.0 - frac_range) * frac_azim, frac_range * frac_azim]
    resampled = jnp.zeros((hidden_two.shape[0], N_AZ * CART_DEV), jnp.float32)
    for k in range(4):
        resampled = resampled + weights[k] * jnp.take(hidden_two, global_cells[k], axis=1).astype(jnp.float32)
    resampled = resampled.astype(jnp.bfloat16)
    group = expand_weight.shape[0] // N_CH
    summed = jnp.zeros((expand_weight.shape[1], N_AZ * CART_DEV), jnp.float32)
    for g in range(N_CH):
        partial_term = lax.dot_general(expand_weight[g * group:(g + 1) * group], resampled[g * group:(g + 1) * group], (((0,), (0,)), ((), ())), preferred_element_type=jnp.float32)
        rounded = lax.optimization_barrier(partial_term.astype(jnp.bfloat16))
        summed = summed + rounded.astype(jnp.float32)
    return (summed + expand_bias[:, None]).astype(jnp.bfloat16)
```

```python
import functools

import jax
import jax.numpy as jnp
from jax import lax
from jax.experimental import pallas as pl
from jax.experimental.pallas import tpu as pltpu
from jax.sharding import PartitionSpec as P

BF16 = jnp.bfloat16
F32 = jnp.float32
VMEM_LIMIT = 48 * 1024 * 1024
DIRECT_TILES = 8


def call(kernel, outs, *args, scratch=(), flops=0, space=None):
    vmem = pl.BlockSpec(memory_space=pltpu.VMEM)
    specs = [
        pl.BlockSpec(memory_space=pltpu.SMEM) if a.ndim == 1 else vmem for a in args
    ]
    touched = sum(a.size * a.dtype.itemsize for a in args)
    touched += sum(o.size * o.dtype.itemsize for o in outs)
    return pl.pallas_call(
        kernel,
        out_shape=tuple(outs),
        in_specs=specs,
        out_specs=tuple(vmem for _ in outs),
        scratch_shapes=list(scratch),
        compiler_params=pltpu.CompilerParams(vmem_limit_bytes=VMEM_LIMIT),
        cost_estimate=pl.CostEstimate(flops=flops, bytes_accessed=touched, transcendentals=0),
    )(*args)


def shape(dims, dtype):
    return jax.ShapeDtypeStruct(dims, dtype)


def range_sum(z, rows):
    length = z.shape[1]
    lane = lax.broadcasted_iota(jnp.int32, (rows, length), 1)
    before = jnp.where(lane == 0, 0.0, pltpu.roll(z[:rows], 1, 1))
    after = jnp.where(lane == length - 1, 0.0, pltpu.roll(z[2 * rows :], length - 1, 1))
    return z[rows : 2 * rows] + before + after


def stack_weights(dest, pieces, places, inputs):
    rows = dest.shape[0] // 3
    share = pieces[0].shape[2]
    for piece, place in zip(pieces, places):
        for i in range(3):
            for j in range(3):
                dest[pl.ds(j * rows + place, share), i * inputs : (i + 1) * inputs] = piece[i, j]


def conv_kernel(
    place, own, halo, w1a, w1b, w1c, w1d, w2a, w2b, pack, keep, send, xs, w1s, hs, w2s
):
    inputs, length = own.shape[0], xs.shape[1]
    core, ch = place[0], place[1]
    columns = own.shape[1] // length
    extra = halo.shape[1] // length
    share = w1a.shape[2]
    total = hs.shape[0] // (xs.shape[0] // inputs - 2)
    for a in range(columns):
        at = pl.multiple_of((a + extra * (1 - core)) * inputs, inputs)
        xs[pl.ds(at, inputs), :] = own[:, a * length : (a + 1) * length]
    for a in range(extra):
        at = pl.multiple_of((a + columns * core) * inputs, inputs)
        xs[pl.ds(at, inputs), :] = halo[:, a * length : (a + 1) * length]
    flips = (0, 1, 2, 3)
    stack_weights(
        w1s,
        (w1a, w1b, w1c, w1d),
        [pl.multiple_of((ch ^ f) * share, share) for f in flips],
        inputs,
    )
    stack_weights(w2s, (w2a, w2b), (0, share), total)
    parts = pack[...].astype(F32)
    bias1 = parts[:, 0:1] + parts[:, 1:2] + parts[:, 2:3]
    hidden_columns = hs.shape[0] // total
    for h in range(hidden_columns):
        z = jnp.dot(
            w1s[...], xs[h * inputs : (h + 3) * inputs, :], preferred_element_type=F32
        )
        value = jnp.maximum(range_sum(z, total) + bias1, 0.0)
        hs[h * total : (h + 1) * total, :] = value.astype(BF16)
    own_at = pl.multiple_of(ch * share, share)
    other_at = pl.multiple_of((ch ^ 1) * share, share)
    bias2 = []
    for at in (own_at, other_at):
        rows = pack[pl.ds(at, share), :].astype(F32)
        bias2.append(rows[:, 3:4] + rows[:, 4:5] + rows[:, 5:6])
    for g in range(hidden_columns - 2):
        z = jnp.dot(w2s[...], hs[g * total : (g + 3) * total, :], preferred_element_type=F32)
        value = range_sum(z, 2 * share)
        lanes = slice(g * length, (g + 1) * length)
        keep[:, lanes] = jnp.maximum(value[:share] + bias2[0], 0.0).astype(BF16)
        send[:, lanes] = jnp.maximum(value[share:] + bias2[1], 0.0).astype(BF16)


def onehot_kernel(place, asked, hot, column, *, length):
    core, turn = place[0], place[1]
    blocks, slots = asked.shape
    for d in range(blocks):
        cells = asked[pl.ds(lax.rem(turn + d, blocks), 1), :]
        row = lax.broadcasted_iota(jnp.int32, (length, slots), 0)
        hot[d] = jnp.where(row == lax.rem(cells, length), 1.0, 0.0).astype(BF16)
        column[d : d + 1, :] = lax.div(cells, length) ^ (2 * core)


def pick_kernel(keep, other, hot, column, *picked):
    share = keep.shape[0]
    length = hot.shape[1]
    groups = []
    for half in (keep, other):
        for a in range(half.shape[1] // length):
            groups.append(half[:, a * length : (a + 1) * length])
    lhs = jnp.concatenate(groups, axis=0)
    for d, out in enumerate(picked):
        z = jnp.dot(lhs, hot[d], preferred_element_type=F32)
        which = column[d : d + 1, :]
        value = z[:share]
        for a in range(1, len(groups)):
            value = jnp.where(which == a, z[a * share : (a + 1) * share], value)
        out[...] = value.astype(BF16)


def sampling_kernel(place, slot, frac, sampling):
    turn, sign = place[0], place[1]
    blocks, slots, cells = sampling.shape
    u, v = frac[0:1, :], frac[1:2, :]
    weights = ((1.0 - u) * (1.0 - v), u * (1.0 - v), (1.0 - u) * v, u * v)
    rows = 64
    places = []
    for k in range(4):
        q = slot[k : k + 1, :]
        block = lax.rem(turn + sign * lax.div(q, slots) + blocks, blocks)
        places.append(block * slots + lax.rem(q, slots))

    def step(n, carry):
        d, r = lax.div(n, slots // rows), lax.rem(n, slots // rows)
        row = lax.broadcasted_iota(jnp.int32, (rows, cells), 0) + n * rows
        value = jnp.zeros((rows, cells), F32)
        for k in range(4):
            value = jnp.where(places[k] == row, weights[k], value)
        sampling[d, pl.ds(pl.multiple_of(r * rows, rows), rows), :] = value.astype(BF16)
        return carry

    lax.fori_loop(0, blocks * slots // rows, step, 0)


def resample_kernel(sampling, *refs):
    arrived, out = refs[:-1], refs[-1]
    total = jnp.zeros(out.shape, F32)
    for d, block in enumerate(arrived):
        total = total + jnp.dot(block[...], sampling[d], preferred_element_type=F32)
    out[...] = total.astype(BF16)


def expand_kernel(weight, resampled, bias, out):
    z = lax.dot_general(
        weight[...], resampled[...], (((0,), (0,)), ((), ())), preferred_element_type=F32
    )
    out[...] = (z + bias[...]).astype(BF16)


def three_parts(value):
    first = value.astype(BF16)
    rest = value - first.astype(F32)
    second = rest.astype(BF16)
    return [first, second, (rest - second.astype(F32)).astype(BF16)]


def local(
    features,
    conv1_weight,
    conv1_bias,
    conv2_weight,
    conv2_bias,
    request_cell,
    corner_slot,
    corner_frac,
    expand_weight,
    expand_bias,
):
    n_az, n_ch = lax.axis_size("az"), lax.axis_size("ch")
    az, ch = lax.axis_index("az"), lax.axis_index("ch")
    core = lax.rem(ch, 2)
    inputs, columns, length = features.shape
    share = conv1_weight.shape[0]
    total = share * n_ch
    cells = corner_slot.shape[1]
    slots = request_cell.shape[0]
    blocks = DIRECT_TILES
    direct = n_az == DIRECT_TILES
    half = columns // 2

    def swap(x, mask):
        return lax.ppermute(x, "ch", [(i, i ^ mask) for i in range(n_ch)])

    pairs = []
    for a in range(n_az):
        for c in range(n_ch):
            to = (a + 1) % n_az if c % 2 == 0 else (a - 1) % n_az
            pairs.append((a * n_ch + c, to * n_ch + c))

    w1 = conv1_weight.transpose(1, 2, 0, 3)
    w2 = conv2_weight.transpose(1, 2, 0, 3)
    w1_y = swap(w1, 2)
    edge = jnp.where(core == 0, features[:, columns - half :], features[:, :half])
    halo = lax.ppermute(edge.reshape(inputs, half * length), ("az", "ch"), pairs)
    own = features.reshape(inputs, columns * length)

    parts = three_parts(conv1_bias) + three_parts(conv2_bias)
    parts = jnp.stack(parts + [jnp.zeros_like(parts[0])] * 2, axis=1)
    parts = jnp.pad(parts, ((0, 0), (0, 120)))
    pack = jnp.concatenate([parts, expand_weight], axis=1)
    pack = jnp.where(core == 0, jnp.stack([pack, swap(pack, 1)]), jnp.stack([swap(pack, 1), pack]))
    pack = pack.reshape(2 * share, -1)
    pack_y = swap(pack, 2)
    pack = jnp.where(ch < 2, jnp.stack([pack, pack_y]), jnp.stack([pack_y, pack]))
    pack = pack.reshape(total, -1)

    asked = lax.all_to_all(
        request_cell.reshape(n_az, -1), "az", split_axis=0, concat_axis=0, tiled=True
    ).reshape(blocks, slots // blocks)

    w1_core = swap(w1, 1)
    w1_far = swap(w1_y, 1)
    w2_core = swap(w2, 1)

    turn = az if direct else jnp.int32(0)
    hot, column = call(
        functools.partial(onehot_kernel, length=length),
        [
            shape((blocks, length, slots // blocks), BF16),
            shape((blocks, slots // blocks), jnp.int32),
        ],
        jnp.stack([core, turn]),
        asked,
    )
    (sampling,) = call(
        sampling_kernel,
        [shape((blocks, slots // blocks, cells), BF16)],
        jnp.stack([turn, jnp.int32(-1 if direct else 1)]),
        corner_slot,
        corner_frac,
    )

    wide = half * length
    keep, send = call(
        conv_kernel,
        [shape((share, wide), BF16)] * 2,
        jnp.stack([core, ch]),
        own,
        halo,
        w1,
        w1_core,
        w1_y,
        w1_far,
        w2,
        w2_core,
        pack[:, :128],
        scratch=[
            pltpu.VMEM(((columns + half) * inputs, length), BF16),
            pltpu.VMEM((3 * total, 3 * inputs), BF16),
            pltpu.VMEM((columns * total, length), BF16),
            pltpu.VMEM((3 * 2 * share, 3 * total), BF16),
        ],
        flops=2 * 9 * inputs * total * columns * length,
    )
    other = swap(send, 1)
    picked = call(
        pick_kernel,
        [shape((share, slots // blocks), BF16)] * blocks,
        keep,
        other,
        hot,
        column,
        flops=2 * share * columns * length * slots,
    )
    if direct:
        arrived = [picked[0]]
        for d in range(1, blocks):
            arrived.append(lax.ppermute(picked[d], "az", [(i, (i + d) % n_az) for i in range(n_az)]))
    else:
        moved = lax.all_to_all(
            jnp.concatenate(picked, axis=1), "az", split_axis=1, concat_axis=1, tiled=True
        )
        arrived = jnp.split(moved, blocks, axis=1)
    (resampled,) = call(
        resample_kernel,
        [shape((share, cells), BF16)],
        sampling,
        *arrived,
        flops=2 * share * slots * cells,
    )
    gathered = lax.all_gather(resampled, "ch", axis=0, tiled=True)
    rows = expand_weight.shape[1] // n_ch
    weight = lax.dynamic_slice_in_dim(pack, 128 + ch * rows, rows, 1)
    (out,) = call(
        expand_kernel,
        [shape((rows, cells), BF16)],
        weight,
        gathered,
        expand_bias.reshape(rows, 1),
        flops=2 * rows * total * cells,
    )
    return out


def solution(mesh):
    return jax.shard_map(
        local,
        mesh=mesh,
        in_specs=(
            P(None, "az", None),
            P("ch", None, None, None),
            P("ch"),
            P("ch", None, None, None),
            P("ch"),
            P("az"),
            P(None, "az"),
            P(None, "az"),
            P("ch", None),
            P("ch"),
        ),
        out_specs=P("ch", "az"),
        check_vma=False,
    )
```

```python
import functools

import jax
import jax.numpy as jnp
from jax import lax
from jax.experimental import pallas as pl
from jax.experimental.pallas import tpu as pltpu
from jax.sharding import PartitionSpec as P

BF16 = jnp.bfloat16
F32 = jnp.float32
VMEM_LIMIT = 48 * 1024 * 1024
TILES = 8


def call(kernel, outs, *args, scratch=(), flops=0, space=None):
    vmem = pl.BlockSpec(memory_space=pltpu.VMEM)
    specs = [
        pl.BlockSpec(memory_space=pltpu.SMEM) if a.ndim == 1 else vmem for a in args
    ]
    touched = sum(a.size * a.dtype.itemsize for a in args)
    touched += sum(o.size * o.dtype.itemsize for o in outs)
    return pl.pallas_call(
        kernel,
        out_shape=tuple(outs),
        in_specs=specs,
        out_specs=tuple(vmem for _ in outs),
        scratch_shapes=list(scratch),
        compiler_params=pltpu.CompilerParams(vmem_limit_bytes=VMEM_LIMIT),
        cost_estimate=pl.CostEstimate(flops=flops, bytes_accessed=touched, transcendentals=0),
    )(*args)


def shape(dims, dtype):
    return jax.ShapeDtypeStruct(dims, dtype)


def range_sum(z, rows):
    length = z.shape[1]
    lane = lax.broadcasted_iota(jnp.int32, (rows, length), 1)
    before = jnp.where(lane == 0, 0.0, pltpu.roll(z[:rows], 1, 1))
    after = jnp.where(lane == length - 1, 0.0, pltpu.roll(z[2 * rows :], length - 1, 1))
    return z[rows : 2 * rows] + before + after


def stack_weights(dest, pieces, places, inputs):
    rows = dest.shape[0] // 3
    share = pieces[0].shape[2]
    for piece, place in zip(pieces, places):
        for i in range(3):
            for j in range(3):
                dest[pl.ds(j * rows + place, share), i * inputs : (i + 1) * inputs] = piece[i, j]


def conv_kernel(place, own, halo, w1a, w1b, w1c, w1d, w2a, w2b, pack, out, xs, w1s, hs, w2s):
    inputs, length = own.shape[0], xs.shape[1]
    core, ch = place[0], place[1]
    columns = own.shape[1] // length
    extra = halo.shape[1] // length
    share = w1a.shape[2]
    total = hs.shape[0] // (xs.shape[0] // inputs - 2)
    for a in range(columns):
        at = pl.multiple_of((a + extra * (1 - core)) * inputs, inputs)
        xs[pl.ds(at, inputs), :] = own[:, a * length : (a + 1) * length]
    for a in range(extra):
        at = pl.multiple_of((a + columns * core) * inputs, inputs)
        xs[pl.ds(at, inputs), :] = halo[:, a * length : (a + 1) * length]
    stack_weights(
        w1s,
        (w1a, w1b, w1c, w1d),
        [pl.multiple_of((ch ^ f) * share, share) for f in range(4)],
        inputs,
    )
    stack_weights(
        w2s, (w2a, w2b), [pl.multiple_of((core ^ f) * share, share) for f in range(2)], total
    )
    parts = pack[...].astype(F32)
    bias1 = parts[:, 0:1] + parts[:, 1:2] + parts[:, 2:3]
    parts = pack[pl.ds(pl.multiple_of((ch - core) * share, 2 * share), 2 * share), :].astype(F32)
    bias2 = parts[:, 3:4] + parts[:, 4:5] + parts[:, 5:6]
    hidden_columns = hs.shape[0] // total
    for h in range(hidden_columns):
        z = jnp.dot(
            w1s[...], xs[h * inputs : (h + 3) * inputs, :], preferred_element_type=F32
        )
        value = jnp.maximum(range_sum(z, total) + bias1, 0.0)
        hs[h * total : (h + 1) * total, :] = value.astype(BF16)
    for g in range(hidden_columns - 2):
        z = jnp.dot(w2s[...], hs[g * total : (g + 3) * total, :], preferred_element_type=F32)
        value = jnp.maximum(range_sum(z, 2 * share) + bias2, 0.0)
        out[:, g * length : (g + 1) * length] = value.astype(BF16)


def onehot_kernel(place, asked, hot, column, *, length, tile_of):
    az, core = place[0], place[1]
    blocks, slots = column.shape
    for m in range(blocks):
        cells = asked[pl.ds(tile_of(az, core, m), 1), :]
        row = lax.broadcasted_iota(jnp.int32, (length, slots), 0)
        hot[m] = jnp.where(row == lax.rem(cells, length), 1.0, 0.0).astype(BF16)
        column[m : m + 1, :] = lax.div(cells, length) ^ (2 * core)


def pick_kernel(mine, other, hot, column, *picked):
    rows = mine.shape[0]
    length = hot.shape[1]
    groups = []
    for half in (mine, other):
        for a in range(half.shape[1] // length):
            groups.append(half[:, a * length : (a + 1) * length])
    lhs = jnp.concatenate(groups, axis=0)
    for m, out in enumerate(picked):
        z = jnp.dot(lhs, hot[m], preferred_element_type=F32)
        which = column[m : m + 1, :]
        value = z[:rows]
        for a in range(1, len(groups)):
            value = jnp.where(which == a, z[a * rows : (a + 1) * rows], value)
        out[...] = value.astype(BF16)


def sampling_kernel(place, slot, frac, sampling, *, block_of):
    az, core = place[0], place[1]
    blocks, slots, cells = sampling.shape
    u, v = frac[0:1, :], frac[1:2, :]
    weights = ((1.0 - u) * (1.0 - v), u * (1.0 - v), (1.0 - u) * v, u * v)
    rows = 64
    places = []
    for k in range(4):
        q = slot[k : k + 1, :]
        block, used = block_of(az, core, lax.div(q, slots))
        places.append(jnp.where(used, block * slots + lax.rem(q, slots), -1))

    def step(n, carry):
        m, r = lax.div(n, slots // rows), lax.rem(n, slots // rows)
        row = lax.broadcasted_iota(jnp.int32, (rows, cells), 0) + n * rows
        value = jnp.zeros((rows, cells), F32)
        for k in range(4):
            value = jnp.where(places[k] == row, weights[k], value)
        sampling[m, pl.ds(pl.multiple_of(r * rows, rows), rows), :] = value.astype(BF16)
        return carry

    lax.fori_loop(0, blocks * slots // rows, step, 0)


def resample_kernel(sampling, *refs):
    arrived, out = refs[:-1], refs[-1]
    total = jnp.zeros(out.shape, F32)
    for m, block in enumerate(arrived):
        total = total + jnp.dot(block[...], sampling[m], preferred_element_type=F32)
    out[...] = total.astype(BF16)


def expand_kernel(place, weight, near_a, near_b, far_a, far_b, bias, out):
    rows = near_a.shape[0]
    plane = place[0]
    near = weight[pl.ds(pl.multiple_of(plane * rows, rows), rows), :]
    far = weight[pl.ds(pl.multiple_of((1 - plane) * rows, rows), rows), :]
    z = bias[...]
    for w, pieces in ((near, (near_a, near_b)), (far, (far_a, far_b))):
        for piece in pieces:
            z = z + lax.dot_general(
                w, piece[...], (((0,), (0,)), ((), ())), preferred_element_type=F32
            )
    out[...] = z.astype(BF16)


def three_parts(value):
    first = value.astype(BF16)
    rest = value - first.astype(F32)
    second = rest.astype(BF16)
    return [first, second, (rest - second.astype(F32)).astype(BF16)]


def local(
    features,
    conv1_weight,
    conv1_bias,
    conv2_weight,
    conv2_bias,
    request_cell,
    corner_slot,
    corner_frac,
    expand_weight,
    expand_bias,
):
    n_az, n_ch = lax.axis_size("az"), lax.axis_size("ch")
    az, ch = lax.axis_index("az"), lax.axis_index("ch")
    core = lax.rem(ch, 2)
    inputs, columns, length = features.shape
    share = conv1_weight.shape[0]
    total = share * n_ch
    cells = corner_slot.shape[1]
    slots = request_cell.shape[0]
    width = slots // TILES
    direct = n_az == TILES
    half = columns // 2

    def swap(x, mask):
        return lax.ppermute(x, "ch", [(i, i ^ mask) for i in range(n_ch)])

    def joint(x, target):
        pairs = []
        for a in range(n_az):
            for c in range(n_ch):
                pairs.append((a * n_ch + c, target(a, c % 2) * n_ch + c))
        return lax.ppermute(x, ("az", "ch"), pairs)

    w1 = conv1_weight.transpose(1, 2, 0, 3)
    w2 = conv2_weight.transpose(1, 2, 0, 3)
    w1_y = swap(w1, 2)
    own = lax.optimization_barrier(features.reshape(inputs, columns * length))
    edge = jnp.where(core == 0, own[:, half * length :], own[:, : half * length])
    halo = joint(edge, lambda a, k: (a + 1 - 2 * k) % n_az)
    edge, request_cell, w1, w2, conv1_bias, conv2_bias, expand_weight = lax.optimization_barrier(
        (edge, request_cell, w1, w2, conv1_bias, conv2_bias, expand_weight)
    )

    asked = lax.all_to_all(
        request_cell.reshape(n_az, -1), "az", split_axis=0, concat_axis=0, tiled=True
    ).reshape(TILES, width)

    parts = three_parts(conv1_bias) + three_parts(conv2_bias)
    parts = jnp.stack(parts + [jnp.zeros_like(parts[0])] * 2, axis=1)
    parts = jnp.pad(parts, ((0, 0), (0, 120)))
    pack = jnp.concatenate([parts, expand_weight], axis=1)
    pack_core = swap(pack, 1)
    pack = jnp.where(core == 0, jnp.stack([pack, pack_core]), jnp.stack([pack_core, pack]))
    pack = pack.reshape(2 * share, -1)
    pack_y = swap(pack, 2)
    pack = jnp.where(ch < 2, jnp.stack([pack, pack_y]), jnp.stack([pack_y, pack]))
    pack = pack.reshape(total, -1)

    w1_core = swap(w1, 1)
    w2_core = swap(w2, 1)
    w1_far = swap(w1_y, 1)

    if direct:
        turns = TILES // 2

        def tile_of(az, core, m):
            return lax.rem(lax.div(az, 2) + m, turns) * 2 + (lax.rem(az, 2) ^ core)

        def block_of(az, core, sector):
            block = lax.rem(lax.div(az, 2) - lax.div(sector, 2) + turns, turns)
            return block, lax.rem(sector, 2) == (lax.rem(az, 2) ^ core)

    else:
        turns = TILES

        def tile_of(az, core, m):
            return m

        def block_of(az, core, sector):
            return sector, sector >= 0

    az_core = jnp.stack([az, core])
    hot, column = call(
        functools.partial(onehot_kernel, length=length, tile_of=tile_of),
        [shape((turns, length, width), BF16), shape((turns, width), jnp.int32)],
        az_core,
        asked,
    )
    (sampling,) = call(
        functools.partial(sampling_kernel, block_of=block_of),
        [shape((turns, width, cells), BF16)],
        az_core,
        corner_slot,
        corner_frac,
    )

    (mine,) = call(
        conv_kernel,
        [shape((2 * share, half * length), BF16)],
        jnp.stack([core, ch]),
        own,
        halo,
        w1,
        w1_core,
        w1_y,
        w1_far,
        w2,
        w2_core,
        pack[:, :128],
        scratch=[
            pltpu.VMEM(((columns + half) * inputs, length), BF16),
            pltpu.VMEM((3 * total, 3 * inputs), BF16),
            pltpu.VMEM((columns * total, length), BF16),
            pltpu.VMEM((3 * 2 * share, 3 * total), BF16),
        ],
        flops=2 * 9 * inputs * total * columns * length,
    )
    other = swap(mine, 1)
    if not direct:
        mine = lax.dynamic_slice_in_dim(mine, core * share, share, 0)
        other = lax.dynamic_slice_in_dim(other, core * share, share, 0)
    rows = mine.shape[0]
    picked = call(
        pick_kernel,
        [shape((rows, width), BF16)] * turns,
        mine,
        other,
        hot,
        column,
        flops=2 * share * columns * length * slots,
    )
    if direct:
        arrived = []
        for m in range(turns):
            arrived.append(
                joint(picked[m], lambda a, k, m=m: (a // 2 + m) % turns * 2 + (a % 2 ^ k))
            )
    else:
        moved = lax.all_to_all(
            jnp.concatenate(picked, axis=1), "az", split_axis=1, concat_axis=1, tiled=True
        )
        arrived = jnp.split(moved, turns, axis=1)
    (near,) = call(
        resample_kernel,
        [shape((rows, cells), BF16)],
        sampling,
        *arrived,
        flops=2 * share * slots * cells,
    )
    if not direct:
        zeros = jnp.zeros_like(near)
        near = jnp.where(core == 0, jnp.stack([near, zeros]), jnp.stack([zeros, near]))
        near = near.reshape(2 * share, cells)
    far = swap(near, 2)
    near_core = swap(near, 1)
    far_core = swap(far, 1)
    outs = expand_weight.shape[1] // n_ch
    weight = lax.dynamic_slice_in_dim(pack, 128 + ch * outs, outs, 1)
    (out,) = call(
        expand_kernel,
        [shape((outs, cells), BF16)],
        lax.div(ch, 2).reshape(1),
        weight,
        near,
        near_core,
        far,
        far_core,
        expand_bias.reshape(outs, 1),
        flops=4 * outs * total * cells,
    )
    return out


def solution(mesh):
    return jax.shard_map(
        local,
        mesh=mesh,
        in_specs=(
            P(None, "az", None),
            P("ch", None, None, None),
            P("ch"),
            P("ch", None, None, None),
            P("ch"),
            P("az"),
            P(None, "az"),
            P(None, "az"),
            P("ch", None),
            P("ch"),
        ),
        out_specs=P("ch", "az"),
        check_vma=False,
    )
```

```python
import functools

import jax
import jax.numpy as jnp
from jax import lax
from jax.experimental import pallas as pl
from jax.experimental.pallas import tpu as pltpu
from jax.sharding import PartitionSpec as P

BF16 = jnp.bfloat16
F32 = jnp.float32
VMEM_LIMIT = 48 * 1024 * 1024
TILES = 8


def call(kernel, outs, *args, scratch=(), flops=0, space=None):
    vmem = pl.BlockSpec(memory_space=pltpu.VMEM)
    specs = [
        pl.BlockSpec(memory_space=pltpu.SMEM) if a.ndim == 1 else vmem for a in args
    ]
    touched = sum(a.size * a.dtype.itemsize for a in args)
    touched += sum(o.size * o.dtype.itemsize for o in outs)
    return pl.pallas_call(
        kernel,
        out_shape=tuple(outs),
        in_specs=specs,
        out_specs=tuple(vmem for _ in outs),
        scratch_shapes=list(scratch),
        compiler_params=pltpu.CompilerParams(vmem_limit_bytes=VMEM_LIMIT),
        cost_estimate=pl.CostEstimate(flops=flops, bytes_accessed=touched, transcendentals=0),
    )(*args)


def shape(dims, dtype):
    return jax.ShapeDtypeStruct(dims, dtype)


def range_sum(z, rows):
    length = z.shape[1]
    lane = lax.broadcasted_iota(jnp.int32, (rows, length), 1)
    before = jnp.where(lane == 0, 0.0, pltpu.roll(z[:rows], 1, 1))
    after = jnp.where(lane == length - 1, 0.0, pltpu.roll(z[2 * rows :], length - 1, 1))
    return z[rows : 2 * rows] + before + after


def stack_weights(dest, pieces, places, inputs):
    rows = dest.shape[0] // 3
    share = pieces[0].shape[2]
    for piece, place in zip(pieces, places):
        for i in range(3):
            for j in range(3):
                dest[pl.ds(j * rows + place, share), i * inputs : (i + 1) * inputs] = piece[i, j]


def prepare_kernel(place, w1a, w1b, w2a, w2b, near, plane):
    core = place[0]
    share = w1a.shape[2]
    places = [pl.multiple_of((core ^ f) * share, share) for f in range(2)]
    stack_weights(near, (w1a, w1b), places, w1a.shape[3])
    stack_weights(plane, (w2a, w2b), places, w2a.shape[3])


def conv_kernel(place, own, halo, near, w2s, w1c, w1d, bias, bias_core, out, xs, far, hs, bs):
    inputs, length = own.shape[0], xs.shape[1]
    core, ch = place[0], place[1]
    columns = own.shape[1] // length
    extra = halo.shape[1] // length
    share = w1c.shape[2]
    total = bs.shape[1]
    for a in range(columns):
        at = pl.multiple_of((a + extra * (1 - core)) * inputs, inputs)
        xs[pl.ds(at, inputs), :] = own[:, a * length : (a + 1) * length]
    for a in range(extra):
        at = pl.multiple_of((a + columns * core) * inputs, inputs)
        xs[pl.ds(at, inputs), :] = halo[:, a * length : (a + 1) * length]
    stack_weights(
        far, (w1c, w1d), [pl.multiple_of((core ^ f) * share, share) for f in range(2)], inputs
    )
    lane = lax.broadcasted_iota(jnp.int32, (share, 2 * share), 1)
    sub = lax.broadcasted_iota(jnp.int32, (share, 2 * share), 0)
    rows = (bias[0:1, :], bias_core[0:1, :], bias[1:2, :], bias_core[1:2, :])
    for f, row in enumerate(rows):
        at = pl.multiple_of((ch ^ f) * share, share)
        for n in range(2):
            column = jnp.sum(jnp.where(lane == sub + n * share, row, 0.0), axis=1, keepdims=True)
            bs[n, pl.ds(at, share), :] = column
    wide = 2 * share
    near_at = pl.multiple_of((ch - core) * share, wide)
    far_at = pl.multiple_of(total - wide - near_at, wide)
    bias2 = bs[1, pl.ds(near_at, wide), :]
    hidden_columns = hs.shape[0] // total
    for weights, at in ((near, near_at), (far, far_at)):
        bias1 = bs[0, pl.ds(at, wide), :]
        for h in range(hidden_columns):
            z = jnp.dot(
                weights[...], xs[h * inputs : (h + 3) * inputs, :], preferred_element_type=F32
            )
            value = jnp.maximum(range_sum(z, wide) + bias1, 0.0)
            hs[pl.ds(pl.multiple_of(h * total + at, wide), wide), :] = value.astype(BF16)
    for g in range(hidden_columns - 2):
        z = jnp.dot(w2s[...], hs[g * total : (g + 3) * total, :], preferred_element_type=F32)
        value = jnp.maximum(range_sum(z, wide) + bias2, 0.0)
        out[:, g * length : (g + 1) * length] = value.astype(BF16)


def table_kernel(asks, slot, frac, table, *, sectors, columns):
    blocks, length = asks.shape
    width = blocks * length // sectors
    lhs = jnp.concatenate(
        [lax.rem(asks[...], length).astype(F32), lax.div(asks[...], length).astype(F32)], axis=0
    ).astype(BF16)
    cells = slot.shape[1]
    high = lax.broadcasted_iota(jnp.int32, (blocks, cells), 0)
    low = lax.broadcasted_iota(jnp.int32, (length, cells), 0)
    for k in range(4):
        q = slot[k : k + 1, :]
        hot = jnp.where(low == lax.rem(q, length), 1.0, 0.0).astype(BF16)
        z = jnp.dot(lhs, hot, preferred_element_type=F32)
        mask = high == lax.div(q, length)
        at = jnp.sum(jnp.where(mask, z[:blocks], 0.0), axis=0, keepdims=True)
        column = jnp.sum(jnp.where(mask, z[blocks:], 0.0), axis=0, keepdims=True)
        sector = lax.div(q, width).astype(F32)
        table[k : k + 1, :] = (sector * columns + column) * length + at
    u, v = frac[0:1, :], frac[1:2, :]
    weights = ((1.0 - u) * (1.0 - v), u * (1.0 - v), (1.0 - u) * v, u * v)
    for k in range(4):
        table[4 + k : 5 + k, :] = weights[k]


def sampling_kernel(place, own, partner, sampling):
    az, core = place[0], place[1]
    blocks, held, both = sampling.shape
    cells = both // 2
    z, x = lax.div(az, 2), lax.rem(az, 2)
    rows = 64
    places, weights = [], []
    for table in (own, partner):
        for k in range(4):
            at = table[k : k + 1, :].astype(jnp.int32)
            sector, cell = lax.div(at, 2 * held), lax.rem(at, 2 * held)
            block = lax.rem(z - lax.div(sector, 2) + blocks, blocks)
            used = (lax.rem(sector, 2) == x) & (lax.div(cell, held) == core)
            places.append(jnp.where(used, block * held + lax.rem(cell, held), -1))
            weights.append(table[4 + k : 5 + k, :])

    def step(n, carry):
        m, r = lax.div(n, held // rows), lax.rem(n, held // rows)
        row = lax.broadcasted_iota(jnp.int32, (rows, cells), 0) + n * rows
        at = pl.ds(pl.multiple_of(r * rows, rows), rows)
        for t in range(2):
            value = jnp.where(places[4 * t] == row, weights[4 * t], 0.0)
            for k in range(4 * t + 1, 4 * t + 4):
                value = value + jnp.where(places[k] == row, weights[k], 0.0)
            sampling[m, at, t * cells : (t + 1) * cells] = value.astype(BF16)
        return carry

    lax.fori_loop(0, blocks * held // rows, step, 0)


def resample_kernel(sampling, *refs):
    held, own, partner = refs[:-2], refs[-2], refs[-1]
    cells = own.shape[1]
    total = jnp.zeros((own.shape[0], 2 * cells), F32)
    for m, block in enumerate(held):
        total = total + jnp.dot(block[...], sampling[m], preferred_element_type=F32)
    own[...] = total[:, :cells].astype(BF16)
    partner[...] = total[:, cells:].astype(BF16)


def expand_kernel(near, far, bias, *refs):
    pieces, out = refs[:-1], refs[-1]
    half = len(pieces) // 2
    z = bias[...]
    for w, group in ((near, pieces[:half]), (far, pieces[half:])):
        for piece in group:
            z = z + lax.dot_general(
                w[...], piece[...], (((0,), (0,)), ((), ())), preferred_element_type=F32
            )
    out[...] = z.astype(BF16)


def sampled_by_request(mine, other, core, request_cell, corner_slot, corner_frac, n_az):
    share = mine.shape[0] // 2
    halves = jnp.where(core == 0, jnp.stack([mine, other]), jnp.stack([other, mine]))
    hidden = lax.dynamic_slice_in_dim(halves, core * share, share, 1)
    hidden = hidden.transpose(1, 0, 2).reshape(share, -1)
    asked = lax.all_to_all(request_cell, "az", split_axis=0, concat_axis=0, tiled=True)
    picked = jnp.take(hidden, asked, axis=1)
    arrived = lax.all_to_all(picked, "az", split_axis=1, concat_axis=1, tiled=True)
    u, v = corner_frac[0][None, :], corner_frac[1][None, :]
    weights = ((1.0 - u) * (1.0 - v), u * (1.0 - v), (1.0 - u) * v, u * v)
    sampled = jnp.zeros((share, corner_slot.shape[1]), F32)
    for k in range(4):
        sampled = sampled + weights[k] * jnp.take(arrived, corner_slot[k], axis=1).astype(F32)
    sampled = sampled.astype(BF16)
    zeros = jnp.zeros_like(sampled)
    placed = jnp.where(core == 0, jnp.stack([sampled, zeros]), jnp.stack([zeros, sampled]))
    return placed.reshape(2 * share, -1)


def local(
    features,
    conv1_weight,
    conv1_bias,
    conv2_weight,
    conv2_bias,
    request_cell,
    corner_slot,
    corner_frac,
    expand_weight,
    expand_bias,
):
    n_az, n_ch = lax.axis_size("az"), lax.axis_size("ch")
    az, ch = lax.axis_index("az"), lax.axis_index("ch")
    core = lax.rem(ch, 2)
    inputs, columns, length = features.shape
    share = conv1_weight.shape[0]
    total = share * n_ch
    cells = corner_slot.shape[1]
    slots = request_cell.shape[0]
    direct = n_az == TILES
    half = columns // 2

    def swap(x, mask):
        return lax.ppermute(x, "ch", [(i, i ^ mask) for i in range(n_ch)])

    def joint(x, target):
        pairs = []
        for a in range(n_az):
            for c in range(n_ch):
                pairs.append((a * n_ch + c, target(a, c % 2) * n_ch + c))
        return lax.ppermute(x, ("az", "ch"), pairs)

    w1 = conv1_weight.transpose(1, 2, 0, 3)
    w2 = conv2_weight.transpose(1, 2, 0, 3)
    w1_y = swap(w1, 2)
    own = lax.optimization_barrier(features.reshape(inputs, columns * length))
    edge = jnp.where(core == 0, own[:, half * length :], own[:, : half * length])
    halo = joint(edge, lambda a, k: (a + 1 - 2 * k) % n_az)
    edge, w1_again, w2_again, conv1_bias, conv2_bias = lax.optimization_barrier(
        (edge, w1, w2, conv1_bias, conv2_bias)
    )

    bias = jnp.concatenate([conv1_bias, conv2_bias]).reshape(1, 2 * share)
    w1_y, bias_y = lax.optimization_barrier((w1_y, swap(bias, 2)))
    bias = jnp.concatenate([bias, bias_y])
    bias, halo = lax.optimization_barrier((bias, halo))
    bias_core = swap(bias, 1)

    w1_far = swap(w1_y, 1)
    w1_core = swap(w1_again, 1)
    w2_core = swap(w2_again, 1)
    w1_near, w2_plane = call(
        prepare_kernel,
        [shape((3 * 2 * share, 3 * inputs), BF16), shape((3 * 2 * share, 3 * total), BF16)],
        core.reshape(1),
        w1,
        w1_core,
        w2,
        w2_core,
    )

    (mine,) = call(
        conv_kernel,
        [shape((2 * share, half * length), BF16)],
        jnp.stack([core, ch]),
        own,
        halo,
        w1_near,
        w2_plane,
        w1_y,
        w1_far,
        bias,
        bias_core,
        scratch=[
            pltpu.VMEM(((columns + half) * inputs, length), BF16),
            pltpu.VMEM((3 * 2 * share, 3 * inputs), BF16),
            pltpu.VMEM((columns * total, length), BF16),
            pltpu.VMEM((2, total, 1), F32),
        ],
        flops=2 * 9 * inputs * total * columns * length,
    )
    outs = expand_weight.shape[1] // n_ch
    expand_weight, mine = lax.optimization_barrier((expand_weight, mine))
    core_rows = swap(expand_weight, 1)
    plane_rows = jnp.where(
        core == 0,
        jnp.stack([expand_weight, core_rows]),
        jnp.stack([core_rows, expand_weight]),
    ).reshape(2 * share, -1)
    weight = lax.dynamic_slice_in_dim(plane_rows, ch * outs, outs, 1)
    weight_y = swap(lax.dynamic_slice_in_dim(plane_rows, (ch ^ 2) * outs, outs, 1), 2)

    if direct:
        turns = TILES // 2
        (table,) = call(
            functools.partial(table_kernel, sectors=n_az, columns=columns),
            [shape((8, cells), F32)],
            request_cell.reshape(-1, length),
            corner_slot,
            corner_frac,
        )
        held = [mine]
        for m in range(1, turns):
            held.append(joint(mine, lambda a, k, m=m: (a + 2 * m) % n_az))
        (sampling,) = call(
            sampling_kernel,
            [shape((turns, half * length, 2 * cells), BF16)],
            jnp.stack([az, core]),
            table,
            joint(table, lambda a, k: a ^ 1),
        )
        held[0], weight, weight_y = lax.optimization_barrier((held[0], weight, weight_y))
        near, partner = call(
            resample_kernel,
            [shape((2 * share, cells), BF16)] * 2,
            sampling,
            *held,
            flops=4 * share * slots * cells,
        )
        nears = [near, joint(partner, lambda a, k: a ^ 1)]
        across = [(a * n_ch + c, (a ^ 1) * n_ch + (c ^ 2)) for a in range(n_az) for c in range(n_ch)]
        fars = [swap(near, 2), lax.ppermute(partner, ("az", "ch"), across)]
    else:
        near = sampled_by_request(
            mine, swap(mine, 1), core, request_cell, corner_slot, corner_frac, n_az
        )
        nears, fars = [near], [swap(near, 2)]
    pieces = nears + [swap(x, 1) for x in nears] + fars + [swap(x, 1) for x in fars]
    (out,) = call(
        expand_kernel,
        [shape((outs, cells), BF16)],
        weight,
        weight_y,
        expand_bias.reshape(outs, 1),
        *pieces,
        flops=4 * outs * total * cells,
    )
    return out


def solution(mesh):
    return jax.shard_map(
        local,
        mesh=mesh,
        in_specs=(
            P(None, "az", None),
            P("ch", None, None, None),
            P("ch"),
            P("ch", None, None, None),
            P("ch"),
            P("az"),
            P(None, "az"),
            P(None, "az"),
            P("ch", None),
            P("ch"),
        ),
        out_specs=P("ch", "az"),
        check_vma=False,
    )
```

```python
import functools

import jax
import jax.numpy as jnp
from jax import lax
from jax.experimental import pallas as pl
from jax.experimental.pallas import tpu as pltpu
from jax.sharding import PartitionSpec as P

BF16 = jnp.bfloat16
F32 = jnp.float32
VMEM_LIMIT = 20 * 1024 * 1024
TILES = 8


def call(kernel, outs, *args, scratch=(), flops=0, left=(), limit=VMEM_LIMIT, touched=None):
    vmem = pl.BlockSpec(memory_space=pltpu.VMEM)
    specs = [
        pl.BlockSpec(memory_space=pltpu.SMEM) if a.ndim == 1 else vmem for a in args
    ]
    for n in left:
        specs[n] = pl.BlockSpec(memory_space=pl.ANY)
    if touched is None:
        touched = sum(a.size * a.dtype.itemsize for a in args)
        touched += sum(o.size * o.dtype.itemsize for o in outs)
    return pl.pallas_call(
        kernel,
        out_shape=tuple(outs),
        in_specs=specs,
        out_specs=tuple(vmem for _ in outs),
        scratch_shapes=list(scratch),
        compiler_params=pltpu.CompilerParams(vmem_limit_bytes=limit),
        cost_estimate=pl.CostEstimate(flops=flops, bytes_accessed=touched, transcendentals=0),
    )(*args)


def shape(dims, dtype):
    return jax.ShapeDtypeStruct(dims, dtype)


def range_sum(z, rows):
    length = z.shape[1]
    lane = lax.broadcasted_iota(jnp.int32, (rows, length), 1)
    before = jnp.where(lane == 0, 0.0, pltpu.roll(z[:rows], 1, 1))
    after = jnp.where(lane == length - 1, 0.0, pltpu.roll(z[2 * rows :], length - 1, 1))
    return z[rows : 2 * rows] + before + after


def stack_weights(dest, pieces, places, inputs):
    rows = dest.shape[0] // 3
    share = pieces[0].shape[2]
    for piece, place in zip(pieces, places):
        for i in range(3):
            for j in range(3):
                dest[pl.ds(j * rows + place, share), i * inputs : (i + 1) * inputs] = piece[i, j]


def edge_kernel(own, edge):
    width = edge.shape[1]
    at = pl.multiple_of((1 - lax.rem(lax.axis_index("ch"), 2)) * width, width)
    edge[...] = own[:, pl.ds(at, width)]


def rows_kernel(wide, rows):
    channels, length = wide.shape[0], rows.shape[1]
    for a in range(rows.shape[0] // channels):
        rows[a * channels : (a + 1) * channels, :] = wide[:, a * length : (a + 1) * length]


def prepare_kernel(place, w1a, w1b, w2a, w2b, near, plane):
    core = place[0]
    share = w1a.shape[2]
    places = [pl.multiple_of((core ^ f) * share, share) for f in range(2)]
    stack_weights(near, (w1a, w1b), places, w1a.shape[3])
    stack_weights(plane, (w2a, w2b), places, w2a.shape[3])


def conv_kernel(place, own, halo, near, w2s, w1c, w1d, bias, bias_core, out, xs, far, hs, bs):
    inputs, length = own.shape[0], xs.shape[1]
    core, ch = place[0], place[1]
    columns = own.shape[1] // length
    extra = halo.shape[0] // inputs
    share = w1c.shape[2]
    total = bs.shape[1]
    for a in range(columns):
        at = pl.multiple_of((a + extra * (1 - core)) * inputs, inputs)
        xs[pl.ds(at, inputs), :] = own[:, a * length : (a + 1) * length]
    for a in range(extra):
        at = pl.multiple_of((a + columns * core) * inputs, inputs)
        xs[pl.ds(at, inputs), :] = halo[a * inputs : (a + 1) * inputs, :]
    stack_weights(
        far, (w1c, w1d), [pl.multiple_of((core ^ f) * share, share) for f in range(2)], inputs
    )
    lane = lax.broadcasted_iota(jnp.int32, (share, 2 * share), 1)
    sub = lax.broadcasted_iota(jnp.int32, (share, 2 * share), 0)
    rows = (bias[0:1, :], bias_core[0:1, :], bias[1:2, :], bias_core[1:2, :])
    for f, row in enumerate(rows):
        at = pl.multiple_of((ch ^ f) * share, share)
        for n in range(2):
            column = jnp.sum(jnp.where(lane == sub + n * share, row, 0.0), axis=1, keepdims=True)
            bs[n, pl.ds(at, share), :] = column
    wide = 2 * share
    near_at = pl.multiple_of((ch - core) * share, wide)
    far_at = pl.multiple_of(total - wide - near_at, wide)
    bias2 = bs[1, pl.ds(near_at, wide), :]
    hidden_columns = hs.shape[0] // total
    for weights, at in ((near, near_at), (far, far_at)):
        bias1 = bs[0, pl.ds(at, wide), :]
        for h in range(hidden_columns):
            z = jnp.dot(
                weights[...], xs[h * inputs : (h + 3) * inputs, :], preferred_element_type=F32
            )
            value = jnp.maximum(range_sum(z, wide) + bias1, 0.0)
            hs[pl.ds(pl.multiple_of(h * total + at, wide), wide), :] = value.astype(BF16)
    for g in range(hidden_columns - 2):
        z = jnp.dot(w2s[...], hs[g * total : (g + 3) * total, :], preferred_element_type=F32)
        value = jnp.maximum(range_sum(z, wide) + bias2, 0.0)
        out[:, g * length : (g + 1) * length] = value.astype(BF16)


def table_kernel(asks, slot, frac, table, *, sectors, columns):
    blocks, length = asks.shape
    width = blocks * length // sectors
    lhs = jnp.concatenate(
        [lax.rem(asks[...], length).astype(F32), lax.div(asks[...], length).astype(F32)], axis=0
    ).astype(BF16)
    cells = slot.shape[1]
    high = lax.broadcasted_iota(jnp.int32, (blocks, cells), 0)
    low = lax.broadcasted_iota(jnp.int32, (length, cells), 0)
    for k in range(4):
        q = slot[k : k + 1, :]
        hot = jnp.where(low == lax.rem(q, length), 1.0, 0.0).astype(BF16)
        z = jnp.dot(lhs, hot, preferred_element_type=F32)
        mask = high == lax.div(q, length)
        at = jnp.sum(jnp.where(mask, z[:blocks], 0.0), axis=0, keepdims=True)
        column = jnp.sum(jnp.where(mask, z[blocks:], 0.0), axis=0, keepdims=True)
        sector = lax.div(q, width).astype(F32)
        table[k : k + 1, :] = (sector * columns + column) * length + at
    u, v = frac[0:1, :], frac[1:2, :]
    weights = ((1.0 - u) * (1.0 - v), u * (1.0 - v), (1.0 - u) * v, u * v)
    for k in range(4):
        table[4 + k : 5 + k, :] = weights[k]


def sampling_kernel(table, sampling):
    az, core = lax.axis_index("az"), lax.rem(lax.axis_index("ch"), 2)
    blocks, held, cells = sampling.shape
    z, x = lax.div(az, 2), lax.rem(az, 2)
    rows = 64
    places, weights = [], []
    for k in range(4):
        at = table[k : k + 1, :].astype(jnp.int32)
        sector, cell = lax.div(at, 2 * held), lax.rem(at, 2 * held)
        block = lax.rem(z - lax.div(sector, 2) + blocks, blocks)
        used = (lax.rem(sector, 2) == x) & (lax.div(cell, held) == core)
        places.append(jnp.where(used, block * held + lax.rem(cell, held), -1))
        weights.append(table[4 + k : 5 + k, :])

    def step(n, carry):
        m, r = lax.div(n, held // rows), lax.rem(n, held // rows)
        row = lax.broadcasted_iota(jnp.int32, (rows, cells), 0) + n * rows
        value = jnp.where(places[0] == row, weights[0], 0.0)
        for k in range(1, 4):
            value = value + jnp.where(places[k] == row, weights[k], 0.0)
        sampling[m, pl.ds(pl.multiple_of(r * rows, rows), rows), :] = value.astype(BF16)
        return carry

    lax.fori_loop(0, blocks * held // rows, step, 0)


def resample_kernel(own, partner, *refs):
    held, kept, sent = refs[:-2], refs[-2], refs[-1]
    first = lax.rem(lax.axis_index("ch"), 2) == 0
    samples = []
    for sampling in (own, partner):
        total = jnp.zeros(kept.shape, F32)
        for m, block in enumerate(held):
            total = total + jnp.dot(block[...], sampling[m], preferred_element_type=F32)
        samples.append(total)
    kept[...] = jnp.where(first, samples[0], samples[1]).astype(BF16)
    sent[...] = jnp.where(first, samples[1], samples[0]).astype(BF16)


def pass_kernel(a, out):
    out[...] = a[...]


def add_kernel(a, b, out):
    out[...] = (a[...].astype(F32) + b[...].astype(F32)).astype(BF16)


def choose_kernel(a, b, out):
    out[...] = jnp.where(lax.rem(lax.axis_index("ch"), 2) == 0, a[...], b[...])


def expand_kernel(wa, wb, wc, wd, bias, *refs):
    pieces, out = [ref[...].astype(F32) for ref in refs[:-1]], refs[-1]
    first = lax.rem(lax.axis_index("ch"), 2) == 0
    near, far = [
        jnp.where(
            first,
            jnp.concatenate([a[...], b[...]], axis=0),
            jnp.concatenate([b[...], a[...]], axis=0),
        )
        for a, b in ((wa, wb), (wc, wd))
    ]
    sums = [pieces[0] + pieces[1], pieces[2] + pieces[3]]
    sums = [value.astype(BF16) for value in sums]
    z = lax.dot_general(
        jnp.concatenate([near, far], axis=0),
        jnp.concatenate(sums, axis=0),
        (((0,), (0,)), ((), ())),
        preferred_element_type=F32,
    )
    out[...] = (z + bias[...]).astype(BF16)


def sampled_by_request(mine, other, core, request_cell, corner_slot, corner_frac, n_az):
    share = mine.shape[0] // 2
    halves = jnp.where(core == 0, jnp.stack([mine, other]), jnp.stack([other, mine]))
    hidden = lax.dynamic_slice_in_dim(halves, core * share, share, 1)
    hidden = hidden.transpose(1, 0, 2).reshape(share, -1)
    asked = lax.all_to_all(request_cell, "az", split_axis=0, concat_axis=0, tiled=True)
    picked = jnp.take(hidden, asked, axis=1)
    arrived = lax.all_to_all(picked, "az", split_axis=1, concat_axis=1, tiled=True)
    u, v = corner_frac[0][None, :], corner_frac[1][None, :]
    weights = ((1.0 - u) * (1.0 - v), u * (1.0 - v), (1.0 - u) * v, u * v)
    sampled = jnp.zeros((share, corner_slot.shape[1]), F32)
    for k in range(4):
        sampled = sampled + weights[k] * jnp.take(arrived, corner_slot[k], axis=1).astype(F32)
    sampled = sampled.astype(BF16)
    zeros = jnp.zeros_like(sampled)
    placed = jnp.where(core == 0, jnp.stack([sampled, zeros]), jnp.stack([zeros, sampled]))
    return placed.reshape(2 * share, -1)


def local(
    features,
    conv1_weight,
    conv1_bias,
    conv2_weight,
    conv2_bias,
    request_cell,
    corner_slot,
    corner_frac,
    expand_weight,
    expand_bias,
):
    n_az, n_ch = lax.axis_size("az"), lax.axis_size("ch")
    az, ch = lax.axis_index("az"), lax.axis_index("ch")
    core = lax.rem(ch, 2)
    inputs, columns, length = features.shape
    share = conv1_weight.shape[0]
    total = share * n_ch
    cells = corner_slot.shape[1]
    slots = request_cell.shape[0]
    direct = n_az == TILES
    half = columns // 2

    def swap(x, mask):
        return lax.ppermute(x, "ch", [(i, i ^ mask) for i in range(n_ch)])

    def joint(x, target):
        pairs = []
        for a in range(n_az):
            for c in range(n_ch):
                pairs.append((a * n_ch + c, target(a, c % 2) * n_ch + c))
        return lax.ppermute(x, ("az", "ch"), pairs)

    w1 = conv1_weight.transpose(1, 2, 0, 3)
    w2 = conv2_weight.transpose(1, 2, 0, 3)
    w1_y = swap(w1, 2)
    own = lax.optimization_barrier(features.reshape(inputs, columns * length))
    (edge,) = call(edge_kernel, [shape((inputs, half * length), BF16)], own, flops=4 * 10**9)
    halo = joint(edge, lambda a, k: (a + 1 - 2 * k) % n_az)
    edge, w1_again, w2_again, conv1_bias, conv2_bias = lax.optimization_barrier(
        (edge, w1, w2, conv1_bias, conv2_bias)
    )

    bias = jnp.concatenate([conv1_bias, conv2_bias]).reshape(1, 2 * share)
    bias_y = swap(bias, 2)
    if direct:
        (table,) = call(
            functools.partial(table_kernel, sectors=n_az, columns=columns),
            [shape((8, cells), F32)],
            request_cell.reshape(-1, length),
            corner_slot,
            corner_frac,
            touched=0,
        )
        w1_y, table = lax.optimization_barrier((w1_y, table))
    w1_y, bias_y = lax.optimization_barrier((w1_y, bias_y))
    bias = jnp.concatenate([bias, bias_y])
    bias_core = swap(bias, 1)

    w1_far = swap(w1_y, 1)
    w1_core = swap(w1_again, 1)
    w2_core = swap(w2_again, 1)
    w1_near, w2_plane = call(
        prepare_kernel,
        [shape((3 * 2 * share, 3 * inputs), BF16), shape((3 * 2 * share, 3 * total), BF16)],
        core.reshape(1),
        w1,
        w1_core,
        w2,
        w2_core,
    )

    (halo,) = call(rows_kernel, [shape((half * inputs, length), BF16)], halo, flops=10**10)
    (mine,) = call(
        conv_kernel,
        [shape((2 * share, half * length), BF16)],
        jnp.stack([core, ch]),
        own,
        halo,
        w1_near,
        w2_plane,
        w1_y,
        w1_far,
        bias,
        bias_core,
        scratch=[
            pltpu.VMEM(((columns + half) * inputs, length), BF16),
            pltpu.VMEM((3 * 2 * share, 3 * inputs), BF16),
            pltpu.VMEM((columns * total, length), BF16),
            pltpu.VMEM((2, total, 1), F32),
        ],
        flops=2 * 9 * inputs * total * columns * length,
    )
    outs = expand_weight.shape[1] // n_ch

    def expansion_slices(expand_weight):
        slices = []
        for f in range(n_ch):
            part = lax.dynamic_slice_in_dim(expand_weight, (ch ^ f) * outs, outs, 1)
            slices.append(swap(part, f) if f else part)
            if f == 1:
                expand_weight, slices[1] = lax.optimization_barrier((expand_weight, slices[1]))
        return slices

    if direct:
        turns = TILES // 2
        mine, table = lax.optimization_barrier((mine, table))
        partner_table = joint(table, lambda a, k: a ^ 1)
        held = [mine]
        for m in range(1, turns):
            held.append(joint(mine, lambda a, k, m=m: (a + 2 * m) % n_az))
        samplings = []
        for entries in (table, partner_table):
            (sampling,) = call(
                sampling_kernel,
                [shape((turns, half * length, cells), BF16)],
                entries,
                touched=0,
            )
            samplings.append(sampling)
        expand_weight, mine = lax.optimization_barrier((expand_weight, mine))
        slices = expansion_slices(expand_weight)
        held[0], slices = lax.optimization_barrier((held[0], slices))
        kept, sent = call(
            resample_kernel,
            [shape((2 * share, cells), BF16)] * 2,
            *samplings,
            *held,
            flops=4 * share * slots * cells,
        )
        tile = shape((2 * share, cells), BF16)
        (kept,) = call(add_kernel, [tile], kept, swap(sent, 1))
        other_plane, same_plane = [], []
        for a in range(n_az):
            for c in range(n_ch):
                other_plane.append((a * n_ch + c, (a ^ (c % 2)) * n_ch + (c ^ 2)))
                if c % 2:
                    same_plane.append((a * n_ch + c, (a ^ 1) * n_ch + c))
        far = lax.ppermute(kept, ("az", "ch"), other_plane)
        (far,) = call(pass_kernel, [tile], far, flops=6 * 10**9)
        near = lax.ppermute(kept, ("az", "ch"), same_plane)
        (near,) = call(choose_kernel, [tile], kept, near)
    else:
        near = sampled_by_request(
            mine, swap(mine, 1), core, request_cell, corner_slot, corner_frac, n_az
        )
        far = swap(near, 2)
        slices = expansion_slices(expand_weight)
    pieces = [near, swap(near, 1), far, swap(far, 1)]
    (out,) = call(
        expand_kernel,
        [shape((outs, cells), BF16)],
        *slices,
        expand_bias.reshape(outs, 1),
        *pieces,
        flops=4 * outs * total * cells,
    )
    return out


def solution(mesh):
    return jax.shard_map(
        local,
        mesh=mesh,
        in_specs=(
            P(None, "az", None),
            P("ch", None, None, None),
            P("ch"),
            P("ch", None, None, None),
            P("ch"),
            P("az"),
            P(None, "az"),
            P(None, "az"),
            P("ch", None),
            P("ch"),
        ),
        out_specs=P("ch", "az"),
        check_vma=False,
    )
```

```python
import functools

import jax
import jax.numpy as jnp
from jax import lax
from jax.experimental import pallas as pl
from jax.experimental.pallas import tpu as pltpu
from jax.sharding import PartitionSpec as P

BF16 = jnp.bfloat16
F32 = jnp.float32
VMEM_LIMIT = 20 * 1024 * 1024
TILES = 8


def call(kernel, outs, *args, scratch=(), flops=0, left=(), limit=VMEM_LIMIT, touched=None):
    vmem = pl.BlockSpec(memory_space=pltpu.VMEM)
    specs = [
        pl.BlockSpec(memory_space=pltpu.SMEM) if a.ndim == 1 else vmem for a in args
    ]
    for n in left:
        specs[n] = pl.BlockSpec(memory_space=pl.ANY)
    if touched is None:
        touched = sum(a.size * a.dtype.itemsize for a in args)
        touched += sum(o.size * o.dtype.itemsize for o in outs)
    return pl.pallas_call(
        kernel,
        out_shape=tuple(outs),
        in_specs=specs,
        out_specs=tuple(vmem for _ in outs),
        scratch_shapes=list(scratch),
        compiler_params=pltpu.CompilerParams(vmem_limit_bytes=limit),
        cost_estimate=pl.CostEstimate(flops=flops, bytes_accessed=touched, transcendentals=0),
    )(*args)


def shape(dims, dtype):
    return jax.ShapeDtypeStruct(dims, dtype)


def range_sum(z, rows):
    length = z.shape[1]
    lane = lax.broadcasted_iota(jnp.int32, (rows, length), 1)
    before = jnp.where(lane == 0, 0.0, pltpu.roll(z[:rows], 1, 1))
    after = jnp.where(lane == length - 1, 0.0, pltpu.roll(z[2 * rows :], length - 1, 1))
    return z[rows : 2 * rows] + before + after


def stack_weights(dest, pieces, places, inputs):
    rows = dest.shape[0] // 3
    share = pieces[0].shape[2]
    for piece, place in zip(pieces, places):
        for i in range(3):
            for j in range(3):
                dest[pl.ds(j * rows + place, share), i * inputs : (i + 1) * inputs] = piece[i, j]


def edge_kernel(own, edge):
    width = edge.shape[1]
    at = pl.multiple_of((1 - lax.rem(lax.axis_index("ch"), 2)) * width, width)
    edge[...] = own[:, pl.ds(at, width)]


def rows_kernel(wide, rows):
    channels, length = wide.shape[0], rows.shape[1]
    for a in range(rows.shape[0] // channels):
        rows[a * channels : (a + 1) * channels, :] = wide[:, a * length : (a + 1) * length]


def prepare_kernel(own, w1a, w1b, w2a, w2b, near, plane, inner, xs):
    core = lax.rem(lax.axis_index("ch"), 2)
    share, inputs, length = w1a.shape[2], w1a.shape[3], xs.shape[1]
    places = [pl.multiple_of((core ^ f) * share, share) for f in range(2)]
    stack_weights(near, (w1a, w1b), places, inputs)
    stack_weights(plane, (w2a, w2b), places, w2a.shape[3])
    for a in range(own.shape[1] // length):
        xs[a * inputs : (a + 1) * inputs, :] = own[:, a * length : (a + 1) * length]
    for n in range(inner.shape[0]):
        z = jnp.dot(near[...], xs[n * inputs : (n + 3) * inputs, :], preferred_element_type=F32)
        inner[n] = range_sum(z, 2 * share)


def conv_kernel(
    own, halo, near, w2s, inner, w1c, w1d, bias, bias_core, out, xs, far, hs, bs
):
    inputs, length = own.shape[0], xs.shape[1]
    ch = lax.axis_index("ch")
    core = lax.rem(ch, 2)
    columns = own.shape[1] // length
    extra = halo.shape[0] // inputs
    share = w1c.shape[2]
    total = bs.shape[1]
    for a in range(columns):
        at = pl.multiple_of((a + extra * (1 - core)) * inputs, inputs)
        xs[pl.ds(at, inputs), :] = own[:, a * length : (a + 1) * length]
    for a in range(extra):
        at = pl.multiple_of((a + columns * core) * inputs, inputs)
        xs[pl.ds(at, inputs), :] = halo[a * inputs : (a + 1) * inputs, :]
    stack_weights(
        far, (w1c, w1d), [pl.multiple_of((core ^ f) * share, share) for f in range(2)], inputs
    )
    lane = lax.broadcasted_iota(jnp.int32, (share, 2 * share), 1)
    sub = lax.broadcasted_iota(jnp.int32, (share, 2 * share), 0)
    rows = (bias[0:1, :], bias_core[0:1, :], bias[1:2, :], bias_core[1:2, :])
    for f, row in enumerate(rows):
        at = pl.multiple_of((ch ^ f) * share, share)
        for n in range(2):
            column = jnp.sum(jnp.where(lane == sub + n * share, row, 0.0), axis=1, keepdims=True)
            bs[n, pl.ds(at, share), :] = column
    wide = 2 * share
    near_at = pl.multiple_of((ch - core) * share, wide)
    far_at = pl.multiple_of(total - wide - near_at, wide)
    bias2 = bs[1, pl.ds(near_at, wide), :]
    hidden_columns = hs.shape[0] // total

    def keep(h, at, value):
        value = jnp.maximum(value + bs[0, pl.ds(at, wide), :], 0.0)
        hs[pl.ds(pl.multiple_of(h * total + at, wide), wide), :] = value.astype(BF16)

    inners = inner.shape[0]
    for n in range(hidden_columns - inners):
        h = n + inners * core
        rows = pl.ds(pl.multiple_of(h * inputs, inputs), 3 * inputs)
        z = jnp.dot(near[...], xs[rows, :], preferred_element_type=F32)
        keep(h, near_at, range_sum(z, wide))
    for n in range(inners):
        keep(n + inners * (1 - core), near_at, inner[n])
    for h in range(hidden_columns):
        z = jnp.dot(far[...], xs[h * inputs : (h + 3) * inputs, :], preferred_element_type=F32)
        keep(h, far_at, range_sum(z, wide))
    for g in range(hidden_columns - 2):
        z = jnp.dot(w2s[...], hs[g * total : (g + 3) * total, :], preferred_element_type=F32)
        value = jnp.maximum(range_sum(z, wide) + bias2, 0.0)
        out[:, g * length : (g + 1) * length] = value.astype(BF16)


def table_kernel(asks, slot, frac, table, *, sectors, columns):
    blocks, length = asks.shape
    width = blocks * length // sectors
    lhs = jnp.concatenate(
        [lax.rem(asks[...], length).astype(F32), lax.div(asks[...], length).astype(F32)], axis=0
    ).astype(BF16)
    cells = slot.shape[1]
    high = lax.broadcasted_iota(jnp.int32, (blocks, cells), 0)
    low = lax.broadcasted_iota(jnp.int32, (length, cells), 0)
    for k in range(4):
        q = slot[k : k + 1, :]
        hot = jnp.where(low == lax.rem(q, length), 1.0, 0.0).astype(BF16)
        z = jnp.dot(lhs, hot, preferred_element_type=F32)
        mask = high == lax.div(q, length)
        at = jnp.sum(jnp.where(mask, z[:blocks], 0.0), axis=0, keepdims=True)
        column = jnp.sum(jnp.where(mask, z[blocks:], 0.0), axis=0, keepdims=True)
        sector = lax.div(q, width).astype(F32)
        table[k : k + 1, :] = (sector * columns + column) * length + at
    u, v = frac[0:1, :], frac[1:2, :]
    weights = ((1.0 - u) * (1.0 - v), u * (1.0 - v), (1.0 - u) * v, u * v)
    for k in range(4):
        table[4 + k : 5 + k, :] = weights[k]


def sampling_kernel(table, sampling):
    az, core = lax.axis_index("az"), lax.rem(lax.axis_index("ch"), 2)
    blocks, held, cells = sampling.shape
    z, x = lax.div(az, 2), lax.rem(az, 2)
    rows = 64
    places, weights = [], []
    for k in range(4):
        at = table[k : k + 1, :].astype(jnp.int32)
        sector, cell = lax.div(at, 2 * held), lax.rem(at, 2 * held)
        block = lax.rem(z - lax.div(sector, 2) + blocks, blocks)
        used = (lax.rem(sector, 2) == x) & (lax.div(cell, held) == core)
        places.append(jnp.where(used, block * held + lax.rem(cell, held), -1))
        weights.append(table[4 + k : 5 + k, :])

    def step(n, carry):
        m, r = lax.div(n, held // rows), lax.rem(n, held // rows)
        row = lax.broadcasted_iota(jnp.int32, (rows, cells), 0) + n * rows
        value = jnp.where(places[0] == row, weights[0], 0.0)
        for k in range(1, 4):
            value = value + jnp.where(places[k] == row, weights[k], 0.0)
        sampling[m, pl.ds(pl.multiple_of(r * rows, rows), rows), :] = value.astype(BF16)
        return carry

    lax.fori_loop(0, blocks * held // rows, step, 0)


def resample_kernel(own, partner, *refs):
    held, kept, sent = refs[:-2], refs[-2], refs[-1]
    first = lax.rem(lax.axis_index("ch"), 2) == 0
    samples = []
    for sampling in (own, partner):
        total = jnp.zeros(kept.shape, F32)
        for m, block in enumerate(held):
            total = total + jnp.dot(block[...], sampling[m], preferred_element_type=F32)
        samples.append(total)
    kept[...] = jnp.where(first, samples[0], samples[1]).astype(BF16)
    sent[...] = jnp.where(first, samples[1], samples[0]).astype(BF16)


def pass_kernel(a, out):
    out[...] = a[...]


def add_kernel(a, b, out):
    out[...] = (a[...].astype(F32) + b[...].astype(F32)).astype(BF16)


def choose_kernel(a, b, out):
    out[...] = jnp.where(lax.rem(lax.axis_index("ch"), 2) == 0, a[...], b[...])


def expand_kernel(wa, wb, wc, wd, bias, *refs):
    pieces, out = [ref[...].astype(F32) for ref in refs[:-1]], refs[-1]
    first = lax.rem(lax.axis_index("ch"), 2) == 0
    near, far = [
        jnp.where(
            first,
            jnp.concatenate([a[...], b[...]], axis=0),
            jnp.concatenate([b[...], a[...]], axis=0),
        )
        for a, b in ((wa, wb), (wc, wd))
    ]
    sums = [pieces[0] + pieces[1], pieces[2] + pieces[3]]
    sums = [value.astype(BF16) for value in sums]
    z = lax.dot_general(
        jnp.concatenate([near, far], axis=0),
        jnp.concatenate(sums, axis=0),
        (((0,), (0,)), ((), ())),
        preferred_element_type=F32,
    )
    out[...] = (z + bias[...]).astype(BF16)


def sampled_by_request(mine, other, core, request_cell, corner_slot, corner_frac, n_az):
    share = mine.shape[0] // 2
    halves = jnp.where(core == 0, jnp.stack([mine, other]), jnp.stack([other, mine]))
    hidden = lax.dynamic_slice_in_dim(halves, core * share, share, 1)
    hidden = hidden.transpose(1, 0, 2).reshape(share, -1)
    asked = lax.all_to_all(request_cell, "az", split_axis=0, concat_axis=0, tiled=True)
    picked = jnp.take(hidden, asked, axis=1)
    arrived = lax.all_to_all(picked, "az", split_axis=1, concat_axis=1, tiled=True)
    u, v = corner_frac[0][None, :], corner_frac[1][None, :]
    weights = ((1.0 - u) * (1.0 - v), u * (1.0 - v), (1.0 - u) * v, u * v)
    sampled = jnp.zeros((share, corner_slot.shape[1]), F32)
    for k in range(4):
        sampled = sampled + weights[k] * jnp.take(arrived, corner_slot[k], axis=1).astype(F32)
    sampled = sampled.astype(BF16)
    zeros = jnp.zeros_like(sampled)
    placed = jnp.where(core == 0, jnp.stack([sampled, zeros]), jnp.stack([zeros, sampled]))
    return placed.reshape(2 * share, -1)


def local(
    features,
    conv1_weight,
    conv1_bias,
    conv2_weight,
    conv2_bias,
    request_cell,
    corner_slot,
    corner_frac,
    expand_weight,
    expand_bias,
):
    n_az, n_ch = lax.axis_size("az"), lax.axis_size("ch")
    az, ch = lax.axis_index("az"), lax.axis_index("ch")
    core = lax.rem(ch, 2)
    inputs, columns, length = features.shape
    share = conv1_weight.shape[0]
    total = share * n_ch
    cells = corner_slot.shape[1]
    slots = request_cell.shape[0]
    direct = n_az == TILES
    half = columns // 2

    def swap(x, mask):
        return lax.ppermute(x, "ch", [(i, i ^ mask) for i in range(n_ch)])

    def joint(x, target):
        pairs = []
        for a in range(n_az):
            for c in range(n_ch):
                pairs.append((a * n_ch + c, target(a, c % 2) * n_ch + c))
        return lax.ppermute(x, ("az", "ch"), pairs)

    w1 = conv1_weight.transpose(1, 2, 0, 3)
    w2 = conv2_weight.transpose(1, 2, 0, 3)
    w1_y = swap(w1, 2)
    own = lax.optimization_barrier(features.reshape(inputs, columns * length))
    (edge,) = call(edge_kernel, [shape((inputs, half * length), BF16)], own, flops=4 * 10**9)
    halo = joint(edge, lambda a, k: (a + 1 - 2 * k) % n_az)
    edge, w1_again, w2_again, conv1_bias, conv2_bias = lax.optimization_barrier(
        (edge, w1, w2, conv1_bias, conv2_bias)
    )

    bias = jnp.concatenate([conv1_bias, conv2_bias]).reshape(1, 2 * share)
    bias_y = swap(bias, 2)
    if direct:
        (table,) = call(
            functools.partial(table_kernel, sectors=n_az, columns=columns),
            [shape((8, cells), F32)],
            request_cell.reshape(-1, length),
            corner_slot,
            corner_frac,
            touched=0,
        )
        w1_y, table = lax.optimization_barrier((w1_y, table))
    w1_y, bias_y = lax.optimization_barrier((w1_y, bias_y))
    bias = jnp.concatenate([bias, bias_y])
    bias_core = swap(bias, 1)

    w1_far = swap(w1_y, 1)
    w1_core = swap(w1_again, 1)
    w2_core = swap(w2_again, 1)
    w1_near, w2_plane, inner = call(
        prepare_kernel,
        [
            shape((3 * 2 * share, 3 * inputs), BF16),
            shape((3 * 2 * share, 3 * total), BF16),
            shape((columns - 2, 2 * share, length), F32),
        ],
        own,
        w1,
        w1_core,
        w2,
        w2_core,
        scratch=[pltpu.VMEM((columns * inputs, length), BF16)],
    )
    (halo,) = call(rows_kernel, [shape((half * inputs, length), BF16)], halo, flops=10**10)
    (mine,) = call(
        conv_kernel,
        [shape((2 * share, half * length), BF16)],
        own,
        halo,
        w1_near,
        w2_plane,
        inner,
        w1_y,
        w1_far,
        bias,
        bias_core,
        scratch=[
            pltpu.VMEM(((columns + half) * inputs, length), BF16),
            pltpu.VMEM((3 * 2 * share, 3 * inputs), BF16),
            pltpu.VMEM((columns * total, length), BF16),
            pltpu.VMEM((2, total, 1), F32),
        ],
        flops=2 * 9 * inputs * total * columns * length,
    )
    outs = expand_weight.shape[1] // n_ch

    def expansion_slices(expand_weight):
        slices = []
        for f in range(n_ch):
            part = lax.dynamic_slice_in_dim(expand_weight, (ch ^ f) * outs, outs, 1)
            slices.append(swap(part, f) if f else part)
            if f == 1:
                expand_weight, slices[1] = lax.optimization_barrier((expand_weight, slices[1]))
        return slices

    if direct:
        turns = TILES // 2
        mine, table = lax.optimization_barrier((mine, table))
        partner_table = joint(table, lambda a, k: a ^ 1)
        held = [mine]
        for m in range(1, turns):
            held.append(joint(mine, lambda a, k, m=m: (a + 2 * m) % n_az))
        samplings = []
        for entries in (table, partner_table):
            (sampling,) = call(
                sampling_kernel,
                [shape((turns, half * length, cells), BF16)],
                entries,
                touched=0,
            )
            samplings.append(sampling)
        expand_weight, mine = lax.optimization_barrier((expand_weight, mine))
        slices = expansion_slices(expand_weight)
        held[0], slices = lax.optimization_barrier((held[0], slices))
        kept, sent = call(
            resample_kernel,
            [shape((2 * share, cells), BF16)] * 2,
            *samplings,
            *held,
            flops=4 * share * slots * cells,
        )
        tile = shape((2 * share, cells), BF16)
        (kept,) = call(add_kernel, [tile], kept, swap(sent, 1))
        other_plane, same_plane = [], []
        for a in range(n_az):
            for c in range(n_ch):
                other_plane.append((a * n_ch + c, (a ^ (c % 2)) * n_ch + (c ^ 2)))
                if c % 2:
                    same_plane.append((a * n_ch + c, (a ^ 1) * n_ch + c))
        far = lax.ppermute(kept, ("az", "ch"), other_plane)
        near = lax.ppermute(kept, ("az", "ch"), same_plane)
        far, near = lax.optimization_barrier((far, near))
        (near,) = call(choose_kernel, [tile], kept, near)
    else:
        near = sampled_by_request(
            mine, swap(mine, 1), core, request_cell, corner_slot, corner_frac, n_az
        )
        far = swap(near, 2)
        slices = expansion_slices(expand_weight)
    pieces = [near, swap(near, 1), far, swap(far, 1)]
    (out,) = call(
        expand_kernel,
        [shape((outs, cells), BF16)],
        *slices,
        expand_bias.reshape(outs, 1),
        *pieces,
        flops=4 * outs * total * cells,
    )
    return out


def solution(mesh):
    return jax.shard_map(
        local,
        mesh=mesh,
        in_specs=(
            P(None, "az", None),
            P("ch", None, None, None),
            P("ch"),
            P("ch", None, None, None),
            P("ch"),
            P("az"),
            P(None, "az"),
            P(None, "az"),
            P("ch", None),
            P("ch"),
        ),
        out_specs=P("ch", "az"),
        check_vma=False,
    )
```

```python
import functools

import jax
import jax.numpy as jnp
from jax import lax
from jax.experimental import pallas as pl
from jax.experimental.pallas import tpu as pltpu
from jax.sharding import PartitionSpec as P

BF16 = jnp.bfloat16
F32 = jnp.float32
VMEM_LIMIT = 20 * 1024 * 1024
TILES = 8


def call(kernel, outs, *args, scratch=(), flops=0, left=(), limit=VMEM_LIMIT, touched=None):
    vmem = pl.BlockSpec(memory_space=pltpu.VMEM)
    specs = [
        pl.BlockSpec(memory_space=pltpu.SMEM) if a.ndim == 1 else vmem for a in args
    ]
    for n in left:
        specs[n] = pl.BlockSpec(memory_space=pl.ANY)
    if touched is None:
        touched = sum(a.size * a.dtype.itemsize for a in args)
        touched += sum(o.size * o.dtype.itemsize for o in outs)
    return pl.pallas_call(
        kernel,
        out_shape=tuple(outs),
        in_specs=specs,
        out_specs=tuple(vmem for _ in outs),
        scratch_shapes=list(scratch),
        compiler_params=pltpu.CompilerParams(vmem_limit_bytes=limit),
        cost_estimate=pl.CostEstimate(flops=flops, bytes_accessed=touched, transcendentals=0),
    )(*args)


def shape(dims, dtype):
    return jax.ShapeDtypeStruct(dims, dtype)


def range_sum(z, rows):
    length = z.shape[1]
    lane = lax.broadcasted_iota(jnp.int32, (rows, length), 1)
    before = jnp.where(lane == 0, 0.0, pltpu.roll(z[:rows], 1, 1))
    after = jnp.where(lane == length - 1, 0.0, pltpu.roll(z[2 * rows :], length - 1, 1))
    return z[rows : 2 * rows] + before + after


def stack_weights(dest, pieces, places, inputs):
    rows = dest.shape[0] // 3
    share = pieces[0].shape[2]
    for piece, place in zip(pieces, places):
        for i in range(3):
            for j in range(3):
                dest[pl.ds(j * rows + place, share), i * inputs : (i + 1) * inputs] = piece[i, j]


def edge_kernel(own, edge):
    width = edge.shape[1]
    at = pl.multiple_of((1 - lax.rem(lax.axis_index("ch"), 2)) * width, width)
    edge[...] = own[:, pl.ds(at, width)]


def rows_kernel(wide, rows):
    channels, length = wide.shape[0], rows.shape[1]
    for a in range(rows.shape[0] // channels):
        rows[a * channels : (a + 1) * channels, :] = wide[:, a * length : (a + 1) * length]


def prepare_kernel(own, w1a, w1b, w2a, w2b, near, plane, inner, xs):
    core = lax.rem(lax.axis_index("ch"), 2)
    share, inputs, length = w1a.shape[2], w1a.shape[3], xs.shape[1]
    places = [pl.multiple_of((core ^ f) * share, share) for f in range(2)]
    stack_weights(near, (w1a, w1b), places, inputs)
    stack_weights(plane, (w2a, w2b), places, w2a.shape[3])
    for a in range(own.shape[1] // length):
        xs[a * inputs : (a + 1) * inputs, :] = own[:, a * length : (a + 1) * length]
    for n in range(inner.shape[0]):
        z = jnp.dot(near[...], xs[n * inputs : (n + 3) * inputs, :], preferred_element_type=F32)
        inner[n] = range_sum(z, 2 * share)


def conv_kernel(
    own, halo, near, w2s, inner, w1c, w1d, bias, bias_core, out, xs, far, hs, bs
):
    inputs, length = own.shape[0], xs.shape[1]
    ch = lax.axis_index("ch")
    core = lax.rem(ch, 2)
    columns = own.shape[1] // length
    extra = halo.shape[0] // inputs
    share = w1c.shape[2]
    total = bs.shape[1]
    for a in range(columns):
        at = pl.multiple_of((a + extra * (1 - core)) * inputs, inputs)
        xs[pl.ds(at, inputs), :] = own[:, a * length : (a + 1) * length]
    for a in range(extra):
        at = pl.multiple_of((a + columns * core) * inputs, inputs)
        xs[pl.ds(at, inputs), :] = halo[a * inputs : (a + 1) * inputs, :]
    stack_weights(
        far, (w1c, w1d), [pl.multiple_of((core ^ f) * share, share) for f in range(2)], inputs
    )
    lane = lax.broadcasted_iota(jnp.int32, (share, 2 * share), 1)
    sub = lax.broadcasted_iota(jnp.int32, (share, 2 * share), 0)
    rows = (bias[0:1, :], bias_core[0:1, :], bias[1:2, :], bias_core[1:2, :])
    for f, row in enumerate(rows):
        at = pl.multiple_of((ch ^ f) * share, share)
        for n in range(2):
            column = jnp.sum(jnp.where(lane == sub + n * share, row, 0.0), axis=1, keepdims=True)
            bs[n, pl.ds(at, share), :] = column
    wide = 2 * share
    near_at = pl.multiple_of((ch - core) * share, wide)
    far_at = pl.multiple_of(total - wide - near_at, wide)
    bias2 = bs[1, pl.ds(near_at, wide), :]
    hidden_columns = hs.shape[0] // total

    def keep(h, at, value):
        value = jnp.maximum(value + bs[0, pl.ds(at, wide), :], 0.0)
        hs[pl.ds(pl.multiple_of(h * total + at, wide), wide), :] = value.astype(BF16)

    inners = inner.shape[0]
    for n in range(hidden_columns - inners):
        h = n + inners * core
        rows = pl.ds(pl.multiple_of(h * inputs, inputs), 3 * inputs)
        z = jnp.dot(near[...], xs[rows, :], preferred_element_type=F32)
        keep(h, near_at, range_sum(z, wide))
    for n in range(inners):
        keep(n + inners * (1 - core), near_at, inner[n])
    for h in range(hidden_columns):
        z = jnp.dot(far[...], xs[h * inputs : (h + 3) * inputs, :], preferred_element_type=F32)
        keep(h, far_at, range_sum(z, wide))
    for g in range(hidden_columns - 2):
        z = jnp.dot(w2s[...], hs[g * total : (g + 3) * total, :], preferred_element_type=F32)
        value = jnp.maximum(range_sum(z, wide) + bias2, 0.0)
        out[:, g * length : (g + 1) * length] = value.astype(BF16)


def table_kernel(asks, slot, frac, table, *, sectors, columns):
    blocks, length = asks.shape
    width = blocks * length // sectors
    lhs = jnp.concatenate(
        [lax.rem(asks[...], length).astype(F32), lax.div(asks[...], length).astype(F32)], axis=0
    ).astype(BF16)
    cells = slot.shape[1]
    high = lax.broadcasted_iota(jnp.int32, (blocks, cells), 0)
    low = lax.broadcasted_iota(jnp.int32, (length, cells), 0)
    for k in range(4):
        q = slot[k : k + 1, :]
        hot = jnp.where(low == lax.rem(q, length), 1.0, 0.0).astype(BF16)
        z = jnp.dot(lhs, hot, preferred_element_type=F32)
        mask = high == lax.div(q, length)
        at = jnp.sum(jnp.where(mask, z[:blocks], 0.0), axis=0, keepdims=True)
        column = jnp.sum(jnp.where(mask, z[blocks:], 0.0), axis=0, keepdims=True)
        sector = lax.div(q, width).astype(F32)
        table[k : k + 1, :] = (sector * columns + column) * length + at
    u, v = frac[0:1, :], frac[1:2, :]
    weights = ((1.0 - u) * (1.0 - v), u * (1.0 - v), (1.0 - u) * v, u * v)
    for k in range(4):
        table[4 + k : 5 + k, :] = weights[k]


def sampling_kernel(table, sampling):
    az, core = lax.axis_index("az"), lax.rem(lax.axis_index("ch"), 2)
    blocks, held, cells = sampling.shape
    z, x = lax.div(az, 2), lax.rem(az, 2)
    rows = 64
    places, weights = [], []
    for k in range(4):
        at = table[k : k + 1, :].astype(jnp.int32)
        sector, cell = lax.div(at, 2 * held), lax.rem(at, 2 * held)
        block = lax.rem(z - lax.div(sector, 2) + blocks, blocks)
        used = (lax.rem(sector, 2) == x) & (lax.div(cell, held) == core)
        places.append(jnp.where(used, block * held + lax.rem(cell, held), -1))
        weights.append(table[4 + k : 5 + k, :])

    def step(n, carry):
        m, r = lax.div(n, held // rows), lax.rem(n, held // rows)
        row = lax.broadcasted_iota(jnp.int32, (rows, cells), 0) + n * rows
        value = jnp.where(places[0] == row, weights[0], 0.0)
        for k in range(1, 4):
            value = value + jnp.where(places[k] == row, weights[k], 0.0)
        sampling[m, pl.ds(pl.multiple_of(r * rows, rows), rows), :] = value.astype(BF16)
        return carry

    lax.fori_loop(0, blocks * held // rows, step, 0)


def resample_kernel(*refs, chosen):
    samplings, held, out = refs[:2], refs[2:-1], refs[-1]
    core = lax.rem(lax.axis_index("ch"), 2)
    for c in range(2):

        @pl.when(core == c)
        def _(sampling=samplings[chosen ^ c]):
            total = jnp.zeros(out.shape, F32)
            for m, block in enumerate(held):
                total = total + jnp.dot(block[...], sampling[m], preferred_element_type=F32)
            out[...] = total.astype(BF16)


def add_kernel(a, b, out):
    out[...] = (a[...].astype(F32) + b[...].astype(F32)).astype(BF16)


def choose_kernel(a, b, out):
    out[...] = jnp.where(lax.rem(lax.axis_index("ch"), 2) == 0, a[...], b[...])


def expand_kernel(wa, wb, wc, wd, bias, *refs):
    pieces, out = [ref[...].astype(F32) for ref in refs[:-1]], refs[-1]
    first = lax.rem(lax.axis_index("ch"), 2) == 0
    near, far = [
        jnp.where(
            first,
            jnp.concatenate([a[...], b[...]], axis=0),
            jnp.concatenate([b[...], a[...]], axis=0),
        )
        for a, b in ((wa, wb), (wc, wd))
    ]
    sums = [pieces[0] + pieces[1], pieces[2] + pieces[3]]
    sums = [value.astype(BF16) for value in sums]
    z = lax.dot_general(
        jnp.concatenate([near, far], axis=0),
        jnp.concatenate(sums, axis=0),
        (((0,), (0,)), ((), ())),
        preferred_element_type=F32,
    )
    out[...] = (z + bias[...]).astype(BF16)


def sampled_by_request(mine, other, core, request_cell, corner_slot, corner_frac, n_az):
    share = mine.shape[0] // 2
    halves = jnp.where(core == 0, jnp.stack([mine, other]), jnp.stack([other, mine]))
    hidden = lax.dynamic_slice_in_dim(halves, core * share, share, 1)
    hidden = hidden.transpose(1, 0, 2).reshape(share, -1)
    asked = lax.all_to_all(request_cell, "az", split_axis=0, concat_axis=0, tiled=True)
    picked = jnp.take(hidden, asked, axis=1)
    arrived = lax.all_to_all(picked, "az", split_axis=1, concat_axis=1, tiled=True)
    u, v = corner_frac[0][None, :], corner_frac[1][None, :]
    weights = ((1.0 - u) * (1.0 - v), u * (1.0 - v), (1.0 - u) * v, u * v)
    sampled = jnp.zeros((share, corner_slot.shape[1]), F32)
    for k in range(4):
        sampled = sampled + weights[k] * jnp.take(arrived, corner_slot[k], axis=1).astype(F32)
    sampled = sampled.astype(BF16)
    zeros = jnp.zeros_like(sampled)
    placed = jnp.where(core == 0, jnp.stack([sampled, zeros]), jnp.stack([zeros, sampled]))
    return placed.reshape(2 * share, -1)


def local(
    features,
    conv1_weight,
    conv1_bias,
    conv2_weight,
    conv2_bias,
    request_cell,
    corner_slot,
    corner_frac,
    expand_weight,
    expand_bias,
):
    n_az, n_ch = lax.axis_size("az"), lax.axis_size("ch")
    az, ch = lax.axis_index("az"), lax.axis_index("ch")
    core = lax.rem(ch, 2)
    inputs, columns, length = features.shape
    share = conv1_weight.shape[0]
    total = share * n_ch
    cells = corner_slot.shape[1]
    slots = request_cell.shape[0]
    direct = n_az == TILES
    half = columns // 2

    def swap(x, mask):
        return lax.ppermute(x, "ch", [(i, i ^ mask) for i in range(n_ch)])

    def joint(x, target):
        pairs = []
        for a in range(n_az):
            for c in range(n_ch):
                pairs.append((a * n_ch + c, target(a, c % 2) * n_ch + c))
        return lax.ppermute(x, ("az", "ch"), pairs)

    w1 = conv1_weight.transpose(1, 2, 0, 3)
    w2 = conv2_weight.transpose(1, 2, 0, 3)
    w1_y = swap(w1, 2)
    own = lax.optimization_barrier(features.reshape(inputs, columns * length))
    (edge,) = call(edge_kernel, [shape((inputs, half * length), BF16)], own, flops=4 * 10**9)
    halo = joint(edge, lambda a, k: (a + 1 - 2 * k) % n_az)
    edge, w1_again, w2_again, conv1_bias, conv2_bias = lax.optimization_barrier(
        (edge, w1, w2, conv1_bias, conv2_bias)
    )

    bias = jnp.concatenate([conv1_bias, conv2_bias]).reshape(1, 2 * share)
    bias_y = swap(bias, 2)
    if direct:
        (table,) = call(
            functools.partial(table_kernel, sectors=n_az, columns=columns),
            [shape((8, cells), F32)],
            request_cell.reshape(-1, length),
            corner_slot,
            corner_frac,
            touched=0,
        )
        w1_y, table = lax.optimization_barrier((w1_y, table))
    w1_y, bias_y = lax.optimization_barrier((w1_y, bias_y))
    bias = jnp.concatenate([bias, bias_y])
    bias_core = swap(bias, 1)

    w1_far = swap(w1_y, 1)
    w1_core = swap(w1_again, 1)
    w2_core = swap(w2_again, 1)
    w1_near, w2_plane, inner = call(
        prepare_kernel,
        [
            shape((3 * 2 * share, 3 * inputs), BF16),
            shape((3 * 2 * share, 3 * total), BF16),
            shape((columns - 2, 2 * share, length), F32),
        ],
        own,
        w1,
        w1_core,
        w2,
        w2_core,
        scratch=[pltpu.VMEM((columns * inputs, length), BF16)],
    )
    (halo,) = call(rows_kernel, [shape((half * inputs, length), BF16)], halo, flops=10**10)
    (mine,) = call(
        conv_kernel,
        [shape((2 * share, half * length), BF16)],
        own,
        halo,
        w1_near,
        w2_plane,
        inner,
        w1_y,
        w1_far,
        bias,
        bias_core,
        scratch=[
            pltpu.VMEM(((columns + half) * inputs, length), BF16),
            pltpu.VMEM((3 * 2 * share, 3 * inputs), BF16),
            pltpu.VMEM((columns * total, length), BF16),
            pltpu.VMEM((2, total, 1), F32),
        ],
        flops=2 * 9 * inputs * total * columns * length,
    )
    outs = expand_weight.shape[1] // n_ch

    def expansion_slices(expand_weight):
        slices = []
        for f in range(n_ch):
            part = lax.dynamic_slice_in_dim(expand_weight, (ch ^ f) * outs, outs, 1)
            slices.append(swap(part, f) if f else part)
            if f == 1:
                expand_weight, slices[1] = lax.optimization_barrier((expand_weight, slices[1]))
        return slices

    if direct:
        turns = TILES // 2
        mine, table = lax.optimization_barrier((mine, table))
        partner_table = joint(table, lambda a, k: a ^ 1)
        held = [mine]
        for m in range(1, turns):
            held.append(joint(mine, lambda a, k, m=m: (a + 2 * m) % n_az))
        samplings = []
        for entries in (table, partner_table):
            (sampling,) = call(
                sampling_kernel,
                [shape((turns, half * length, cells), BF16)],
                entries,
                touched=0,
            )
            samplings.append(sampling)
        expand_weight, mine = lax.optimization_barrier((expand_weight, mine))
        slices = expansion_slices(expand_weight)
        held[0], slices = lax.optimization_barrier((held[0], slices))
        tile = shape((2 * share, cells), BF16)
        sent, kept = [
            call(
                functools.partial(resample_kernel, chosen=chosen),
                [tile],
                *samplings,
                *held,
                flops=2 * share * slots * cells,
            )[0]
            for chosen in (1, 0)
        ]
        (kept,) = call(add_kernel, [tile], kept, swap(sent, 1))
        other_plane, same_plane = [], []
        for a in range(n_az):
            for c in range(n_ch):
                other_plane.append((a * n_ch + c, (a ^ (c % 2)) * n_ch + (c ^ 2)))
                if c % 2:
                    same_plane.append((a * n_ch + c, (a ^ 1) * n_ch + c))
        far = lax.ppermute(kept, ("az", "ch"), other_plane)
        near = lax.ppermute(kept, ("az", "ch"), same_plane)
        far, near = lax.optimization_barrier((far, near))
        (near,) = call(choose_kernel, [tile], kept, near)
    else:
        near = sampled_by_request(
            mine, swap(mine, 1), core, request_cell, corner_slot, corner_frac, n_az
        )
        far = swap(near, 2)
        slices = expansion_slices(expand_weight)
    pieces = [near, swap(near, 1), far, swap(far, 1)]
    (out,) = call(
        expand_kernel,
        [shape((outs, cells), BF16)],
        *slices,
        expand_bias.reshape(outs, 1),
        *pieces,
        flops=4 * outs * total * cells,
    )
    return out


def solution(mesh):
    return jax.shard_map(
        local,
        mesh=mesh,
        in_specs=(
            P(None, "az", None),
            P("ch", None, None, None),
            P("ch"),
            P("ch", None, None, None),
            P("ch"),
            P("az"),
            P(None, "az"),
            P(None, "az"),
            P("ch", None),
            P("ch"),
        ),
        out_specs=P("ch", "az"),
        check_vma=False,
    )
```

```python
import functools

import jax
import jax.numpy as jnp
from jax import lax
from jax.experimental import pallas as pl
from jax.experimental.pallas import tpu as pltpu
from jax.sharding import PartitionSpec as P

BF16 = jnp.bfloat16
F32 = jnp.float32
VMEM_LIMIT = 20 * 1024 * 1024
TILES = 8


def call(kernel, outs, *args, scratch=(), flops=0, touched=None):
    vmem = pl.BlockSpec(memory_space=pltpu.VMEM)
    if touched is None:
        touched = sum(a.size * a.dtype.itemsize for a in args)
        touched += sum(o.size * o.dtype.itemsize for o in outs)
    return pl.pallas_call(
        kernel,
        out_shape=tuple(outs),
        in_specs=[vmem] * len(args),
        out_specs=tuple(vmem for _ in outs),
        scratch_shapes=list(scratch),
        compiler_params=pltpu.CompilerParams(vmem_limit_bytes=VMEM_LIMIT),
        cost_estimate=pl.CostEstimate(flops=flops, bytes_accessed=touched, transcendentals=0),
    )(*args)


def shape(dims, dtype):
    return jax.ShapeDtypeStruct(dims, dtype)


def range_sum(z, rows):
    length = z.shape[1]
    lane = lax.broadcasted_iota(jnp.int32, (rows, length), 1)
    before = jnp.where(lane == 0, 0.0, pltpu.roll(z[:rows], 1, 1))
    after = jnp.where(lane == length - 1, 0.0, pltpu.roll(z[2 * rows :], length - 1, 1))
    return z[rows : 2 * rows] + before + after


def stack_weights(dest, pieces, places, inputs):
    rows = dest.shape[0] // 3
    share = pieces[0].shape[2]
    for piece, place in zip(pieces, places):
        for i in range(3):
            for j in range(3):
                dest[pl.ds(j * rows + place, share), i * inputs : (i + 1) * inputs] = piece[i, j]


def edge_kernel(own, edge):
    width = edge.shape[1]
    at = pl.multiple_of((1 - lax.rem(lax.axis_index("ch"), 2)) * width, width)
    edge[...] = own[:, pl.ds(at, width)]


def rows_kernel(wide, rows):
    channels, length = wide.shape[0], rows.shape[1]
    for a in range(rows.shape[0] // channels):
        rows[a * channels : (a + 1) * channels, :] = wide[:, a * length : (a + 1) * length]


def prepare_kernel(own, w1a, w1b, w2a, w2b, near, plane, inner, xs):
    core = lax.rem(lax.axis_index("ch"), 2)
    share, inputs, length = w1a.shape[2], w1a.shape[3], xs.shape[1]
    places = [pl.multiple_of((core ^ f) * share, share) for f in range(2)]
    stack_weights(near, (w1a, w1b), places, inputs)
    stack_weights(plane, (w2a, w2b), places, w2a.shape[3])
    for a in range(own.shape[1] // length):
        xs[a * inputs : (a + 1) * inputs, :] = own[:, a * length : (a + 1) * length]
    for n in range(inner.shape[0]):
        z = jnp.dot(near[...], xs[n * inputs : (n + 3) * inputs, :], preferred_element_type=F32)
        inner[n] = range_sum(z, 2 * share)


def conv_kernel(
    own, halo, near, w2s, inner, w1c, w1d, bias, bias_core, out, xs, far, hs, bs
):
    inputs, length = own.shape[0], xs.shape[1]
    ch = lax.axis_index("ch")
    core = lax.rem(ch, 2)
    columns = own.shape[1] // length
    extra = halo.shape[0] // inputs
    share = w1c.shape[2]
    total = bs.shape[1]
    for a in range(columns):
        at = pl.multiple_of((a + extra * (1 - core)) * inputs, inputs)
        xs[pl.ds(at, inputs), :] = own[:, a * length : (a + 1) * length]
    for a in range(extra):
        at = pl.multiple_of((a + columns * core) * inputs, inputs)
        xs[pl.ds(at, inputs), :] = halo[a * inputs : (a + 1) * inputs, :]
    stack_weights(
        far, (w1c, w1d), [pl.multiple_of((core ^ f) * share, share) for f in range(2)], inputs
    )
    lane = lax.broadcasted_iota(jnp.int32, (share, 2 * share), 1)
    sub = lax.broadcasted_iota(jnp.int32, (share, 2 * share), 0)
    rows = (bias[0:1, :], bias_core[0:1, :], bias[1:2, :], bias_core[1:2, :])
    for f, row in enumerate(rows):
        at = pl.multiple_of((ch ^ f) * share, share)
        for n in range(2):
            column = jnp.sum(jnp.where(lane == sub + n * share, row, 0.0), axis=1, keepdims=True)
            bs[n, pl.ds(at, share), :] = column
    wide = 2 * share
    near_at = pl.multiple_of((ch - core) * share, wide)
    far_at = pl.multiple_of(total - wide - near_at, wide)
    bias2 = bs[1, pl.ds(near_at, wide), :]
    hidden_columns = hs.shape[0] // total

    def keep(h, at, value):
        value = jnp.maximum(value + bs[0, pl.ds(at, wide), :], 0.0)
        hs[pl.ds(pl.multiple_of(h * total + at, wide), wide), :] = value.astype(BF16)

    inners = inner.shape[0]
    for n in range(hidden_columns - inners):
        h = n + inners * core
        rows = pl.ds(pl.multiple_of(h * inputs, inputs), 3 * inputs)
        z = jnp.dot(near[...], xs[rows, :], preferred_element_type=F32)
        keep(h, near_at, range_sum(z, wide))
    for n in range(inners):
        keep(n + inners * (1 - core), near_at, inner[n])
    for h in range(hidden_columns):
        z = jnp.dot(far[...], xs[h * inputs : (h + 3) * inputs, :], preferred_element_type=F32)
        keep(h, far_at, range_sum(z, wide))
    for g in range(hidden_columns - 2):
        z = jnp.dot(w2s[...], hs[g * total : (g + 3) * total, :], preferred_element_type=F32)
        value = jnp.maximum(range_sum(z, wide) + bias2, 0.0)
        out[:, g * length : (g + 1) * length] = value.astype(BF16)


def table_kernel(asks, slot, frac, table, *, sectors, columns):
    blocks, length = asks.shape
    width = blocks * length // sectors
    lhs = jnp.concatenate(
        [lax.rem(asks[...], length).astype(F32), lax.div(asks[...], length).astype(F32)], axis=0
    ).astype(BF16)
    cells = slot.shape[1]
    high = lax.broadcasted_iota(jnp.int32, (blocks, cells), 0)
    low = lax.broadcasted_iota(jnp.int32, (length, cells), 0)
    for k in range(4):
        q = slot[k : k + 1, :]
        hot = jnp.where(low == lax.rem(q, length), 1.0, 0.0).astype(BF16)
        z = jnp.dot(lhs, hot, preferred_element_type=F32)
        mask = high == lax.div(q, length)
        at = jnp.sum(jnp.where(mask, z[:blocks], 0.0), axis=0, keepdims=True)
        column = jnp.sum(jnp.where(mask, z[blocks:], 0.0), axis=0, keepdims=True)
        sector = lax.div(q, width).astype(F32)
        table[k : k + 1, :] = (sector * columns + column) * length + at
    u, v = frac[0:1, :], frac[1:2, :]
    weights = ((1.0 - u) * (1.0 - v), u * (1.0 - v), (1.0 - u) * v, u * v)
    for k in range(4):
        table[4 + k : 5 + k, :] = weights[k]


def sampling_kernel(table, sampling):
    az, core = lax.axis_index("az"), lax.rem(lax.axis_index("ch"), 2)
    blocks, held, cells = sampling.shape
    z, x = lax.div(az, 2), lax.rem(az, 2)
    rows = 64
    places, weights = [], []
    for k in range(4):
        at = table[k : k + 1, :].astype(jnp.int32)
        sector, cell = lax.div(at, 2 * held), lax.rem(at, 2 * held)
        block = lax.rem(z - lax.div(sector, 2) + blocks, blocks)
        used = (lax.rem(sector, 2) == x) & (lax.div(cell, held) == core)
        places.append(jnp.where(used, block * held + lax.rem(cell, held), -1))
        weights.append(table[4 + k : 5 + k, :])

    def step(n, carry):
        m, r = lax.div(n, held // rows), lax.rem(n, held // rows)
        row = lax.broadcasted_iota(jnp.int32, (rows, cells), 0) + n * rows
        value = jnp.where(places[0] == row, weights[0], 0.0)
        for k in range(1, 4):
            value = value + jnp.where(places[k] == row, weights[k], 0.0)
        sampling[m, pl.ds(pl.multiple_of(r * rows, rows), rows), :] = value.astype(BF16)
        return carry

    lax.fori_loop(0, blocks * held // rows, step, 0)


def resample_kernel(*refs, chosen):
    samplings, held, out = refs[:2], refs[2:-1], refs[-1]
    core = lax.rem(lax.axis_index("ch"), 2)
    for c in range(2):

        @pl.when(core == c)
        def _(sampling=samplings[chosen ^ c]):
            total = jnp.zeros(out.shape, F32)
            for m, block in enumerate(held):
                total = total + jnp.dot(block[...], sampling[m], preferred_element_type=F32)
            out[...] = total.astype(BF16)


def add_kernel(a, b, out):
    out[...] = (a[...].astype(F32) + b[...].astype(F32)).astype(BF16)


def choose_kernel(a, b, out):
    out[...] = jnp.where(lax.rem(lax.axis_index("ch"), 2) == 0, a[...], b[...])


def expand_kernel(wa, wb, wc, wd, bias, *refs):
    pieces, out = [ref[...].astype(F32) for ref in refs[:-1]], refs[-1]
    first = lax.rem(lax.axis_index("ch"), 2) == 0
    near, far = [
        jnp.where(
            first,
            jnp.concatenate([a[...], b[...]], axis=0),
            jnp.concatenate([b[...], a[...]], axis=0),
        )
        for a, b in ((wa, wb), (wc, wd))
    ]
    sums = [pieces[0] + pieces[1], pieces[2] + pieces[3]]
    sums = [value.astype(BF16) for value in sums]
    z = lax.dot_general(
        jnp.concatenate([near, far], axis=0),
        jnp.concatenate(sums, axis=0),
        (((0,), (0,)), ((), ())),
        preferred_element_type=F32,
    )
    out[...] = (z + bias[...]).astype(BF16)


def sampled_by_request(mine, other, core, request_cell, corner_slot, corner_frac, n_az):
    share = mine.shape[0] // 2
    halves = jnp.where(core == 0, jnp.stack([mine, other]), jnp.stack([other, mine]))
    hidden = lax.dynamic_slice_in_dim(halves, core * share, share, 1)
    hidden = hidden.transpose(1, 0, 2).reshape(share, -1)
    asked = lax.all_to_all(request_cell, "az", split_axis=0, concat_axis=0, tiled=True)
    picked = jnp.take(hidden, asked, axis=1)
    arrived = lax.all_to_all(picked, "az", split_axis=1, concat_axis=1, tiled=True)
    u, v = corner_frac[0][None, :], corner_frac[1][None, :]
    weights = ((1.0 - u) * (1.0 - v), u * (1.0 - v), (1.0 - u) * v, u * v)
    sampled = jnp.zeros((share, corner_slot.shape[1]), F32)
    for k in range(4):
        sampled = sampled + weights[k] * jnp.take(arrived, corner_slot[k], axis=1).astype(F32)
    sampled = sampled.astype(BF16)
    zeros = jnp.zeros_like(sampled)
    placed = jnp.where(core == 0, jnp.stack([sampled, zeros]), jnp.stack([zeros, sampled]))
    return placed.reshape(2 * share, -1)


def local(
    features,
    conv1_weight,
    conv1_bias,
    conv2_weight,
    conv2_bias,
    request_cell,
    corner_slot,
    corner_frac,
    expand_weight,
    expand_bias,
):
    n_az, n_ch = lax.axis_size("az"), lax.axis_size("ch")
    az, ch = lax.axis_index("az"), lax.axis_index("ch")
    core = lax.rem(ch, 2)
    inputs, columns, length = features.shape
    share = conv1_weight.shape[0]
    total = share * n_ch
    cells = corner_slot.shape[1]
    slots = request_cell.shape[0]
    direct = n_az == TILES
    half = columns // 2

    def swap(x, mask):
        return lax.ppermute(x, "ch", [(i, i ^ mask) for i in range(n_ch)])

    def joint(x, target):
        pairs = []
        for a in range(n_az):
            for c in range(n_ch):
                pairs.append((a * n_ch + c, target(a, c % 2) * n_ch + c))
        return lax.ppermute(x, ("az", "ch"), pairs)

    w1 = conv1_weight.transpose(1, 2, 0, 3)
    w2 = conv2_weight.transpose(1, 2, 0, 3)
    w1_y = swap(w1, 2)
    own = lax.optimization_barrier(features.reshape(inputs, columns * length))
    (edge,) = call(edge_kernel, [shape((inputs, half * length), BF16)], own, flops=4 * 10**9)
    halo = joint(edge, lambda a, k: (a + 1 - 2 * k) % n_az)
    edge, w1_again, w2_again, conv1_bias, conv2_bias = lax.optimization_barrier(
        (edge, w1, w2, conv1_bias, conv2_bias)
    )

    bias = jnp.concatenate([conv1_bias, conv2_bias]).reshape(1, 2 * share)
    bias_y = swap(bias, 2)
    if direct:
        (table,) = call(
            functools.partial(table_kernel, sectors=n_az, columns=columns),
            [shape((8, cells), F32)],
            request_cell.reshape(-1, length),
            corner_slot,
            corner_frac,
            touched=0,
        )
        w1_y, table = lax.optimization_barrier((w1_y, table))
    w1_y, bias_y = lax.optimization_barrier((w1_y, bias_y))
    bias = jnp.concatenate([bias, bias_y])
    bias_core = swap(bias, 1)

    w1_far = swap(w1_y, 1)
    w1_core = swap(w1_again, 1)
    w2_core = swap(w2_again, 1)
    w1_near, w2_plane, inner = call(
        prepare_kernel,
        [
            shape((3 * 2 * share, 3 * inputs), BF16),
            shape((3 * 2 * share, 3 * total), BF16),
            shape((columns - 2, 2 * share, length), F32),
        ],
        own,
        w1,
        w1_core,
        w2,
        w2_core,
        scratch=[pltpu.VMEM((columns * inputs, length), BF16)],
    )
    (halo,) = call(rows_kernel, [shape((half * inputs, length), BF16)], halo, flops=10**10)
    (mine,) = call(
        conv_kernel,
        [shape((2 * share, half * length), BF16)],
        own,
        halo,
        w1_near,
        w2_plane,
        inner,
        w1_y,
        w1_far,
        bias,
        bias_core,
        scratch=[
            pltpu.VMEM(((columns + half) * inputs, length), BF16),
            pltpu.VMEM((3 * 2 * share, 3 * inputs), BF16),
            pltpu.VMEM((columns * total, length), BF16),
            pltpu.VMEM((2, total, 1), F32),
        ],
        flops=2 * 9 * inputs * total * columns * length,
    )
    outs = expand_weight.shape[1] // n_ch

    def expansion_slices(expand_weight):
        slices = []
        for f in range(n_ch):
            part = lax.dynamic_slice_in_dim(expand_weight, (ch ^ f) * outs, outs, 1)
            slices.append(swap(part, f) if f else part)
        return slices

    if direct:
        turns = TILES // 2
        mine, table = lax.optimization_barrier((mine, table))
        partner_table = joint(table, lambda a, k: a ^ 1)
        held = [mine]
        for m in range(1, turns):
            held.append(joint(mine, lambda a, k, m=m: (a + 2 * m) % n_az))
        expand_weight, partner_table = lax.optimization_barrier((expand_weight, partner_table))
        samplings = []
        for entries in (table, partner_table):
            (sampling,) = call(
                sampling_kernel,
                [shape((turns, half * length, cells), BF16)],
                entries,
                touched=0,
            )
            samplings.append(sampling)
        slices = expansion_slices(expand_weight)
        held[0], slices = lax.optimization_barrier((held[0], slices))
        tile = shape((2 * share, cells), BF16)
        sent, kept = [
            call(
                functools.partial(resample_kernel, chosen=chosen),
                [tile],
                *samplings,
                *held,
                flops=2 * share * slots * cells,
            )[0]
            for chosen in (1, 0)
        ]
        (kept,) = call(add_kernel, [tile], kept, swap(sent, 1))
        other_plane, same_plane = [], []
        for a in range(n_az):
            for c in range(n_ch):
                other_plane.append((a * n_ch + c, (a ^ (c % 2)) * n_ch + (c ^ 2)))
                if c % 2:
                    same_plane.append((a * n_ch + c, (a ^ 1) * n_ch + c))
        far = lax.ppermute(kept, ("az", "ch"), other_plane)
        near = lax.ppermute(kept, ("az", "ch"), same_plane)
        far, near = lax.optimization_barrier((far, near))
        (near,) = call(choose_kernel, [tile], kept, near)
    else:
        near = sampled_by_request(
            mine, swap(mine, 1), core, request_cell, corner_slot, corner_frac, n_az
        )
        far = swap(near, 2)
        slices = expansion_slices(expand_weight)
    pieces = [near, swap(near, 1), far, swap(far, 1)]
    (out,) = call(
        expand_kernel,
        [shape((outs, cells), BF16)],
        *slices,
        expand_bias.reshape(outs, 1),
        *pieces,
        flops=4 * outs * total * cells,
    )
    return out


def solution(mesh):
    return jax.shard_map(
        local,
        mesh=mesh,
        in_specs=(
            P(None, "az", None),
            P("ch", None, None, None),
            P("ch"),
            P("ch", None, None, None),
            P("ch"),
            P("az"),
            P(None, "az"),
            P(None, "az"),
            P("ch", None),
            P("ch"),
        ),
        out_specs=P("ch", "az"),
        check_vma=False,
    )
```

```python
import functools

import jax
import jax.numpy as jnp
from jax import lax
from jax.experimental import pallas as pl
from jax.experimental.pallas import tpu as pltpu
from jax.sharding import PartitionSpec as P

BF16 = jnp.bfloat16
F32 = jnp.float32
VMEM_LIMIT = 20 * 1024 * 1024
TILES = 8


def call(kernel, outs, *args, scratch=(), flops=0, touched=None):
    vmem = pl.BlockSpec(memory_space=pltpu.VMEM)
    if touched is None:
        touched = sum(a.size * a.dtype.itemsize for a in args)
        touched += sum(o.size * o.dtype.itemsize for o in outs)
    return pl.pallas_call(
        kernel,
        out_shape=tuple(outs),
        in_specs=[vmem] * len(args),
        out_specs=tuple(vmem for _ in outs),
        scratch_shapes=list(scratch),
        compiler_params=pltpu.CompilerParams(vmem_limit_bytes=VMEM_LIMIT),
        cost_estimate=pl.CostEstimate(flops=flops, bytes_accessed=touched, transcendentals=0),
    )(*args)


def shape(dims, dtype):
    return jax.ShapeDtypeStruct(dims, dtype)


def range_sum(z, rows):
    length = z.shape[1]
    lane = lax.broadcasted_iota(jnp.int32, (rows, length), 1)
    before = jnp.where(lane == 0, 0.0, pltpu.roll(z[:rows], 1, 1))
    after = jnp.where(lane == length - 1, 0.0, pltpu.roll(z[2 * rows :], length - 1, 1))
    return z[rows : 2 * rows] + before + after


def stack_weights(dest, pieces, places, inputs):
    rows = dest.shape[0] // 3
    share = pieces[0].shape[2]
    for piece, place in zip(pieces, places):
        for i in range(3):
            for j in range(3):
                dest[pl.ds(j * rows + place, share), i * inputs : (i + 1) * inputs] = piece[i, j]


def edge_kernel(own, edge):
    width = edge.shape[1]
    at = pl.multiple_of((1 - lax.rem(lax.axis_index("ch"), 2)) * width, width)
    edge[...] = own[:, pl.ds(at, width)]


def rows_kernel(wide, rows):
    channels, length = wide.shape[0], rows.shape[1]
    for a in range(rows.shape[0] // channels):
        rows[a * channels : (a + 1) * channels, :] = wide[:, a * length : (a + 1) * length]


def own_rows_kernel(own, weight, xs, stack, inner):
    share, inputs, length = weight.shape[2], weight.shape[3], xs.shape[1]
    for i in range(3):
        for j in range(3):
            stack[j * share : (j + 1) * share, i * inputs : (i + 1) * inputs] = weight[i, j]
    for a in range(own.shape[1] // length):
        xs[a * inputs : (a + 1) * inputs, :] = own[:, a * length : (a + 1) * length]
    for n in range(inner.shape[0]):
        z = jnp.dot(stack[...], xs[n * inputs : (n + 3) * inputs, :], preferred_element_type=F32)
        inner[n] = range_sum(z, share)


def prepare_kernel(xs, own_stack, own_inner, w1b, w2a, w2b, near, plane, inner, stack):
    core = lax.rem(lax.axis_index("ch"), 2)
    share, inputs = w1b.shape[2], w1b.shape[3]
    places = [pl.multiple_of((core ^ f) * share, share) for f in range(2)]
    stack_weights(plane, (w2a, w2b), places, w2a.shape[3])
    for i in range(3):
        for j in range(3):
            stack[j * share : (j + 1) * share, i * inputs : (i + 1) * inputs] = w1b[i, j]
    for j in range(3):
        rows = slice(j * share, (j + 1) * share)
        for source, place in zip((own_stack, stack), places):
            near[pl.ds(2 * j * share + place, share), :] = source[rows, :]
    for n in range(inner.shape[0]):
        z = jnp.dot(stack[...], xs[n * inputs : (n + 3) * inputs, :], preferred_element_type=F32)
        inner[n, pl.ds(places[0], share), :] = own_inner[n]
        inner[n, pl.ds(places[1], share), :] = range_sum(z, share)


def conv_kernel(
    own, halo, near, w2s, inner, w1c, w1d, bias, bias_core, out, xs, far, hs, bs
):
    inputs, length = own.shape[0], xs.shape[1]
    ch = lax.axis_index("ch")
    core = lax.rem(ch, 2)
    columns = own.shape[1] // length
    extra = halo.shape[0] // inputs
    share = w1c.shape[2]
    total = bs.shape[1]
    for a in range(columns):
        at = pl.multiple_of((a + extra * (1 - core)) * inputs, inputs)
        xs[pl.ds(at, inputs), :] = own[:, a * length : (a + 1) * length]
    for a in range(extra):
        at = pl.multiple_of((a + columns * core) * inputs, inputs)
        xs[pl.ds(at, inputs), :] = halo[a * inputs : (a + 1) * inputs, :]
    stack_weights(
        far, (w1c, w1d), [pl.multiple_of((core ^ f) * share, share) for f in range(2)], inputs
    )
    lane = lax.broadcasted_iota(jnp.int32, (share, 2 * share), 1)
    sub = lax.broadcasted_iota(jnp.int32, (share, 2 * share), 0)
    rows = (bias[0:1, :], bias_core[0:1, :], bias[1:2, :], bias_core[1:2, :])
    for f, row in enumerate(rows):
        at = pl.multiple_of((ch ^ f) * share, share)
        for n in range(2):
            column = jnp.sum(jnp.where(lane == sub + n * share, row, 0.0), axis=1, keepdims=True)
            bs[n, pl.ds(at, share), :] = column
    wide = 2 * share
    near_at = pl.multiple_of((ch - core) * share, wide)
    far_at = pl.multiple_of(total - wide - near_at, wide)
    bias2 = bs[1, pl.ds(near_at, wide), :]
    hidden_columns = hs.shape[0] // total

    def keep(h, at, value):
        value = jnp.maximum(value + bs[0, pl.ds(at, wide), :], 0.0)
        hs[pl.ds(pl.multiple_of(h * total + at, wide), wide), :] = value.astype(BF16)

    inners = inner.shape[0]
    for n in range(hidden_columns - inners):
        h = n + inners * core
        rows = pl.ds(pl.multiple_of(h * inputs, inputs), 3 * inputs)
        z = jnp.dot(near[...], xs[rows, :], preferred_element_type=F32)
        keep(h, near_at, range_sum(z, wide))
    for n in range(inners):
        keep(n + inners * (1 - core), near_at, inner[n])
    for h in range(hidden_columns):
        z = jnp.dot(far[...], xs[h * inputs : (h + 3) * inputs, :], preferred_element_type=F32)
        keep(h, far_at, range_sum(z, wide))
    for g in range(hidden_columns - 2):
        z = jnp.dot(w2s[...], hs[g * total : (g + 3) * total, :], preferred_element_type=F32)
        value = jnp.maximum(range_sum(z, wide) + bias2, 0.0)
        out[:, g * length : (g + 1) * length] = value.astype(BF16)


def table_kernel(asks, slot, frac, table, *, sectors, columns):
    blocks, length = asks.shape
    width = blocks * length // sectors
    lhs = jnp.concatenate(
        [lax.rem(asks[...], length).astype(F32), lax.div(asks[...], length).astype(F32)], axis=0
    ).astype(BF16)
    cells = slot.shape[1]
    high = lax.broadcasted_iota(jnp.int32, (blocks, cells), 0)
    low = lax.broadcasted_iota(jnp.int32, (length, cells), 0)
    for k in range(4):
        q = slot[k : k + 1, :]
        hot = jnp.where(low == lax.rem(q, length), 1.0, 0.0).astype(BF16)
        z = jnp.dot(lhs, hot, preferred_element_type=F32)
        mask = high == lax.div(q, length)
        at = jnp.sum(jnp.where(mask, z[:blocks], 0.0), axis=0, keepdims=True)
        column = jnp.sum(jnp.where(mask, z[blocks:], 0.0), axis=0, keepdims=True)
        sector = lax.div(q, width).astype(F32)
        table[k : k + 1, :] = (sector * columns + column) * length + at
    u, v = frac[0:1, :], frac[1:2, :]
    weights = ((1.0 - u) * (1.0 - v), u * (1.0 - v), (1.0 - u) * v, u * v)
    for k in range(4):
        table[4 + k : 5 + k, :] = weights[k]


def sampling_kernel(table, sampling):
    az, core = lax.axis_index("az"), lax.rem(lax.axis_index("ch"), 2)
    blocks, held, cells = sampling.shape
    z, x = lax.div(az, 2), lax.rem(az, 2)
    rows = 64
    places, weights = [], []
    for k in range(4):
        at = table[k : k + 1, :].astype(jnp.int32)
        sector, cell = lax.div(at, 2 * held), lax.rem(at, 2 * held)
        block = lax.rem(z - lax.div(sector, 2) + blocks, blocks)
        used = (lax.rem(sector, 2) == x) & (lax.div(cell, held) == core)
        places.append(jnp.where(used, block * held + lax.rem(cell, held), -1))
        weights.append(table[4 + k : 5 + k, :])

    def step(n, carry):
        m, r = lax.div(n, held // rows), lax.rem(n, held // rows)
        row = lax.broadcasted_iota(jnp.int32, (rows, cells), 0) + n * rows
        value = jnp.where(places[0] == row, weights[0], 0.0)
        for k in range(1, 4):
            value = value + jnp.where(places[k] == row, weights[k], 0.0)
        sampling[m, pl.ds(pl.multiple_of(r * rows, rows), rows), :] = value.astype(BF16)
        return carry

    lax.fori_loop(0, blocks * held // rows, step, 0)


def resample_kernel(*refs, chosen):
    samplings, held, out = refs[:2], refs[2:-1], refs[-1]
    core = lax.rem(lax.axis_index("ch"), 2)
    for c in range(2):

        @pl.when(core == c)
        def _(sampling=samplings[chosen ^ c]):
            total = jnp.zeros(out.shape, F32)
            for m, block in enumerate(held):
                total = total + jnp.dot(block[...], sampling[m], preferred_element_type=F32)
            out[...] = total.astype(BF16)


def add_kernel(a, b, out):
    out[...] = (a[...].astype(F32) + b[...].astype(F32)).astype(BF16)


def choose_kernel(a, b, out):
    out[...] = jnp.where(lax.rem(lax.axis_index("ch"), 2) == 0, a[...], b[...])


def expand_kernel(wa, wb, wc, wd, bias, *refs):
    pieces, out = [ref[...].astype(F32) for ref in refs[:-1]], refs[-1]
    first = lax.rem(lax.axis_index("ch"), 2) == 0
    near, far = [
        jnp.where(
            first,
            jnp.concatenate([a[...], b[...]], axis=0),
            jnp.concatenate([b[...], a[...]], axis=0),
        )
        for a, b in ((wa, wb), (wc, wd))
    ]
    sums = [pieces[0] + pieces[1], pieces[2] + pieces[3]]
    sums = [value.astype(BF16) for value in sums]
    z = lax.dot_general(
        jnp.concatenate([near, far], axis=0),
        jnp.concatenate(sums, axis=0),
        (((0,), (0,)), ((), ())),
        preferred_element_type=F32,
    )
    out[...] = (z + bias[...]).astype(BF16)


def sampled_by_request(mine, other, core, request_cell, corner_slot, corner_frac, n_az):
    share = mine.shape[0] // 2
    halves = jnp.where(core == 0, jnp.stack([mine, other]), jnp.stack([other, mine]))
    hidden = lax.dynamic_slice_in_dim(halves, core * share, share, 1)
    hidden = hidden.transpose(1, 0, 2).reshape(share, -1)
    asked = lax.all_to_all(request_cell, "az", split_axis=0, concat_axis=0, tiled=True)
    picked = jnp.take(hidden, asked, axis=1)
    arrived = lax.all_to_all(picked, "az", split_axis=1, concat_axis=1, tiled=True)
    u, v = corner_frac[0][None, :], corner_frac[1][None, :]
    weights = ((1.0 - u) * (1.0 - v), u * (1.0 - v), (1.0 - u) * v, u * v)
    sampled = jnp.zeros((share, corner_slot.shape[1]), F32)
    for k in range(4):
        sampled = sampled + weights[k] * jnp.take(arrived, corner_slot[k], axis=1).astype(F32)
    sampled = sampled.astype(BF16)
    zeros = jnp.zeros_like(sampled)
    placed = jnp.where(core == 0, jnp.stack([sampled, zeros]), jnp.stack([zeros, sampled]))
    return placed.reshape(2 * share, -1)


def local(
    features,
    conv1_weight,
    conv1_bias,
    conv2_weight,
    conv2_bias,
    request_cell,
    corner_slot,
    corner_frac,
    expand_weight,
    expand_bias,
):
    n_az, n_ch = lax.axis_size("az"), lax.axis_size("ch")
    az, ch = lax.axis_index("az"), lax.axis_index("ch")
    core = lax.rem(ch, 2)
    inputs, columns, length = features.shape
    share = conv1_weight.shape[0]
    total = share * n_ch
    cells = corner_slot.shape[1]
    slots = request_cell.shape[0]
    direct = n_az == TILES
    half = columns // 2

    def swap(x, mask):
        return lax.ppermute(x, "ch", [(i, i ^ mask) for i in range(n_ch)])

    def joint(x, target):
        pairs = []
        for a in range(n_az):
            for c in range(n_ch):
                pairs.append((a * n_ch + c, target(a, c % 2) * n_ch + c))
        return lax.ppermute(x, ("az", "ch"), pairs)

    w1 = conv1_weight.transpose(1, 2, 0, 3)
    w2 = conv2_weight.transpose(1, 2, 0, 3)
    w1_y = swap(w1, 2)
    own = lax.optimization_barrier(features.reshape(inputs, columns * length))
    (edge,) = call(edge_kernel, [shape((inputs, half * length), BF16)], own, flops=4 * 10**9)
    halo = joint(edge, lambda a, k: (a + 1 - 2 * k) % n_az)
    edge, w1_again, w2_again, conv1_bias, conv2_bias = lax.optimization_barrier(
        (edge, w1, w2, conv1_bias, conv2_bias)
    )

    bias = jnp.concatenate([conv1_bias, conv2_bias]).reshape(1, 2 * share)
    bias_y = swap(bias, 2)
    if direct:
        (table,) = call(
            functools.partial(table_kernel, sectors=n_az, columns=columns),
            [shape((8, cells), F32)],
            request_cell.reshape(-1, length),
            corner_slot,
            corner_frac,
            touched=0,
        )
        w1_y, table = lax.optimization_barrier((w1_y, table))
    own_rows, own_stack, own_inner = call(
        own_rows_kernel,
        [
            shape((columns * inputs, length), BF16),
            shape((3 * share, 3 * inputs), BF16),
            shape((columns - 2, share, length), F32),
        ],
        own,
        w1,
        touched=0,
    )
    w1_y, bias_y, own_inner = lax.optimization_barrier((w1_y, bias_y, own_inner))
    bias = jnp.concatenate([bias, bias_y])
    bias_core = swap(bias, 1)

    w1_far = swap(w1_y, 1)
    w1_core = swap(w1_again, 1)
    w2_core = swap(w2_again, 1)
    w1_near, w2_plane, inner = call(
        prepare_kernel,
        [
            shape((3 * 2 * share, 3 * inputs), BF16),
            shape((3 * 2 * share, 3 * total), BF16),
            shape((columns - 2, 2 * share, length), F32),
        ],
        own_rows,
        own_stack,
        own_inner,
        w1_core,
        w2,
        w2_core,
        scratch=[pltpu.VMEM((3 * share, 3 * inputs), BF16)],
    )
    (halo,) = call(rows_kernel, [shape((half * inputs, length), BF16)], halo, flops=10**10)
    (mine,) = call(
        conv_kernel,
        [shape((2 * share, half * length), BF16)],
        own,
        halo,
        w1_near,
        w2_plane,
        inner,
        w1_y,
        w1_far,
        bias,
        bias_core,
        scratch=[
            pltpu.VMEM(((columns + half) * inputs, length), BF16),
            pltpu.VMEM((3 * 2 * share, 3 * inputs), BF16),
            pltpu.VMEM((columns * total, length), BF16),
            pltpu.VMEM((2, total, 1), F32),
        ],
        flops=2 * 9 * inputs * total * columns * length,
    )
    outs = expand_weight.shape[1] // n_ch

    def expansion_slices(expand_weight):
        slices = []
        for f in range(n_ch):
            part = lax.dynamic_slice_in_dim(expand_weight, (ch ^ f) * outs, outs, 1)
            slices.append(swap(part, f) if f else part)
        return slices

    if direct:
        turns = TILES // 2
        mine, table = lax.optimization_barrier((mine, table))
        partner_table = joint(table, lambda a, k: a ^ 1)
        held = [mine]
        for m in range(1, turns):
            held.append(joint(mine, lambda a, k, m=m: (a + 2 * m) % n_az))
        expand_weight, partner_table = lax.optimization_barrier((expand_weight, partner_table))
        samplings = []
        for entries in (table, partner_table):
            (sampling,) = call(
                sampling_kernel,
                [shape((turns, half * length, cells), BF16)],
                entries,
                touched=0,
            )
            samplings.append(sampling)
        slices = expansion_slices(expand_weight)
        held[0], slices = lax.optimization_barrier((held[0], slices))
        tile = shape((2 * share, cells), BF16)
        sent, kept = [
            call(
                functools.partial(resample_kernel, chosen=chosen),
                [tile],
                *samplings,
                *held,
                flops=2 * share * slots * cells,
            )[0]
            for chosen in (1, 0)
        ]
        (kept,) = call(add_kernel, [tile], kept, swap(sent, 1))
        other_plane, same_plane = [], []
        for a in range(n_az):
            for c in range(n_ch):
                other_plane.append((a * n_ch + c, (a ^ (c % 2)) * n_ch + (c ^ 2)))
                if c % 2:
                    same_plane.append((a * n_ch + c, (a ^ 1) * n_ch + c))
        far = lax.ppermute(kept, ("az", "ch"), other_plane)
        near = lax.ppermute(kept, ("az", "ch"), same_plane)
        far, near = lax.optimization_barrier((far, near))
        (near,) = call(choose_kernel, [tile], kept, near)
    else:
        near = sampled_by_request(
            mine, swap(mine, 1), core, request_cell, corner_slot, corner_frac, n_az
        )
        far = swap(near, 2)
        slices = expansion_slices(expand_weight)
    pieces = [near, swap(near, 1), far, swap(far, 1)]
    (out,) = call(
        expand_kernel,
        [shape((outs, cells), BF16)],
        *slices,
        expand_bias.reshape(outs, 1),
        *pieces,
        flops=4 * outs * total * cells,
    )
    return out


def solution(mesh):
    return jax.shard_map(
        local,
        mesh=mesh,
        in_specs=(
            P(None, "az", None),
            P("ch", None, None, None),
            P("ch"),
            P("ch", None, None, None),
            P("ch"),
            P("az"),
            P(None, "az"),
            P(None, "az"),
            P("ch", None),
            P("ch"),
        ),
        out_specs=P("ch", "az"),
        check_vma=False,
    )
```

```python
import functools

import jax
import jax.numpy as jnp
from jax import lax
from jax.experimental import pallas as pl
from jax.experimental.pallas import tpu as pltpu
from jax.sharding import PartitionSpec as P

BF16 = jnp.bfloat16
F32 = jnp.float32
VMEM_LIMIT = 20 * 1024 * 1024
TILES = 8


def call(kernel, outs, *args, scratch=(), flops=0, touched=None):
    vmem = pl.BlockSpec(memory_space=pltpu.VMEM)
    if touched is None:
        touched = sum(a.size * a.dtype.itemsize for a in args)
        touched += sum(o.size * o.dtype.itemsize for o in outs)
    return pl.pallas_call(
        kernel,
        out_shape=tuple(outs),
        in_specs=[vmem] * len(args),
        out_specs=tuple(vmem for _ in outs),
        scratch_shapes=list(scratch),
        compiler_params=pltpu.CompilerParams(vmem_limit_bytes=VMEM_LIMIT),
        cost_estimate=pl.CostEstimate(flops=flops, bytes_accessed=touched, transcendentals=0),
    )(*args)


def shape(dims, dtype):
    return jax.ShapeDtypeStruct(dims, dtype)


def range_sum(z, rows):
    length = z.shape[1]
    lane = lax.broadcasted_iota(jnp.int32, (rows, length), 1)
    before = jnp.where(lane == 0, 0.0, pltpu.roll(z[:rows], 1, 1))
    after = jnp.where(lane == length - 1, 0.0, pltpu.roll(z[2 * rows :], length - 1, 1))
    return z[rows : 2 * rows] + before + after


def stack_weights(dest, pieces, places, inputs):
    rows = dest.shape[0] // 3
    share = pieces[0].shape[2]
    for piece, place in zip(pieces, places):
        for i in range(3):
            for j in range(3):
                dest[pl.ds(j * rows + place, share), i * inputs : (i + 1) * inputs] = piece[i, j]


def edge_kernel(own, edge):
    width = edge.shape[1]
    at = pl.multiple_of((1 - lax.rem(lax.axis_index("ch"), 2)) * width, width)
    edge[...] = own[:, pl.ds(at, width)]


def rows_kernel(wide, rows):
    channels, length = wide.shape[0], rows.shape[1]
    for a in range(rows.shape[0] // channels):
        rows[a * channels : (a + 1) * channels, :] = wide[:, a * length : (a + 1) * length]


def own_rows_kernel(own, weight, xs, stack, inner):
    share, inputs, length = weight.shape[2], weight.shape[3], xs.shape[1]
    for i in range(3):
        for j in range(3):
            stack[j * share : (j + 1) * share, i * inputs : (i + 1) * inputs] = weight[i, j]
    for a in range(own.shape[1] // length):
        xs[a * inputs : (a + 1) * inputs, :] = own[:, a * length : (a + 1) * length]
    for n in range(inner.shape[0]):
        z = jnp.dot(stack[...], xs[n * inputs : (n + 3) * inputs, :], preferred_element_type=F32)
        inner[n] = range_sum(z, share)


def prepare_kernel(xs, own_stack, own_inner, w1b, w2a, w2b, near, plane, inner, stack):
    core = lax.rem(lax.axis_index("ch"), 2)
    share, inputs = w1b.shape[2], w1b.shape[3]
    places = [pl.multiple_of((core ^ f) * share, share) for f in range(2)]
    stack_weights(plane, (w2a, w2b), places, w2a.shape[3])
    for i in range(3):
        for j in range(3):
            stack[j * share : (j + 1) * share, i * inputs : (i + 1) * inputs] = w1b[i, j]
    for j in range(3):
        rows = slice(j * share, (j + 1) * share)
        for source, place in zip((own_stack, stack), places):
            near[pl.ds(2 * j * share + place, share), :] = source[rows, :]
    for n in range(inner.shape[0]):
        z = jnp.dot(stack[...], xs[n * inputs : (n + 3) * inputs, :], preferred_element_type=F32)
        inner[n, pl.ds(places[0], share), :] = own_inner[n]
        inner[n, pl.ds(places[1], share), :] = range_sum(z, share)


def conv_kernel(
    own, halo, near, w2s, inner, w1c, w1d, bias, bias_core, out, xs, far, hs, bs
):
    inputs, length = own.shape[0], xs.shape[1]
    ch = lax.axis_index("ch")
    core = lax.rem(ch, 2)
    columns = own.shape[1] // length
    extra = halo.shape[0] // inputs
    share = w1c.shape[2]
    total = bs.shape[1]
    for a in range(columns):
        at = pl.multiple_of((a + extra * (1 - core)) * inputs, inputs)
        xs[pl.ds(at, inputs), :] = own[:, a * length : (a + 1) * length]
    for a in range(extra):
        at = pl.multiple_of((a + columns * core) * inputs, inputs)
        xs[pl.ds(at, inputs), :] = halo[a * inputs : (a + 1) * inputs, :]
    stack_weights(
        far, (w1c, w1d), [pl.multiple_of((core ^ f) * share, share) for f in range(2)], inputs
    )
    lane = lax.broadcasted_iota(jnp.int32, (share, 2 * share), 1)
    sub = lax.broadcasted_iota(jnp.int32, (share, 2 * share), 0)
    rows = (bias[0:1, :], bias_core[0:1, :], bias[1:2, :], bias_core[1:2, :])
    for f, row in enumerate(rows):
        at = pl.multiple_of((ch ^ f) * share, share)
        for n in range(2):
            column = jnp.sum(jnp.where(lane == sub + n * share, row, 0.0), axis=1, keepdims=True)
            bs[n, pl.ds(at, share), :] = column
    wide = 2 * share
    near_at = pl.multiple_of((ch - core) * share, wide)
    far_at = pl.multiple_of(total - wide - near_at, wide)
    bias2 = bs[1, pl.ds(near_at, wide), :]
    hidden_columns = hs.shape[0] // total

    def keep(h, at, value):
        value = jnp.maximum(value + bs[0, pl.ds(at, wide), :], 0.0)
        hs[pl.ds(pl.multiple_of(h * total + at, wide), wide), :] = value.astype(BF16)

    inners = inner.shape[0]
    for n in range(hidden_columns - inners):
        h = n + inners * core
        rows = pl.ds(pl.multiple_of(h * inputs, inputs), 3 * inputs)
        z = jnp.dot(near[...], xs[rows, :], preferred_element_type=F32)
        keep(h, near_at, range_sum(z, wide))
    for n in range(inners):
        keep(n + inners * (1 - core), near_at, inner[n])
    for h in range(hidden_columns):
        z = jnp.dot(far[...], xs[h * inputs : (h + 3) * inputs, :], preferred_element_type=F32)
        keep(h, far_at, range_sum(z, wide))
    for g in range(hidden_columns - 2):
        z = jnp.dot(w2s[...], hs[g * total : (g + 3) * total, :], preferred_element_type=F32)
        value = jnp.maximum(range_sum(z, wide) + bias2, 0.0)
        out[:, g * length : (g + 1) * length] = value.astype(BF16)


def table_kernel(asks, slot, frac, table, *, sectors, columns):
    blocks, length = asks.shape
    width = blocks * length // sectors
    lhs = jnp.concatenate(
        [lax.rem(asks[...], length).astype(F32), lax.div(asks[...], length).astype(F32)], axis=0
    ).astype(BF16)
    cells = slot.shape[1]
    high = lax.broadcasted_iota(jnp.int32, (blocks, cells), 0)
    low = lax.broadcasted_iota(jnp.int32, (length, cells), 0)
    for k in range(4):
        q = slot[k : k + 1, :]
        hot = jnp.where(low == lax.rem(q, length), 1.0, 0.0).astype(BF16)
        z = jnp.dot(lhs, hot, preferred_element_type=F32)
        mask = high == lax.div(q, length)
        at = jnp.sum(jnp.where(mask, z[:blocks], 0.0), axis=0, keepdims=True)
        column = jnp.sum(jnp.where(mask, z[blocks:], 0.0), axis=0, keepdims=True)
        sector = lax.div(q, width).astype(F32)
        table[k : k + 1, :] = (sector * columns + column) * length + at
    u, v = frac[0:1, :], frac[1:2, :]
    weights = ((1.0 - u) * (1.0 - v), u * (1.0 - v), (1.0 - u) * v, u * v)
    for k in range(4):
        table[4 + k : 5 + k, :] = weights[k]


def sampling_kernel(table, sampling):
    az, core = lax.axis_index("az"), lax.rem(lax.axis_index("ch"), 2)
    blocks, held, cells = sampling.shape
    z, x = lax.div(az, 2), lax.rem(az, 2)
    rows = 64
    places, weights = [], []
    for k in range(4):
        at = table[k : k + 1, :].astype(jnp.int32)
        sector, cell = lax.div(at, 2 * held), lax.rem(at, 2 * held)
        block = lax.rem(z - lax.div(sector, 2) + blocks, blocks)
        used = (lax.rem(sector, 2) == x) & (lax.div(cell, held) == core)
        places.append(jnp.where(used, block * held + lax.rem(cell, held), -1))
        weights.append(table[4 + k : 5 + k, :])

    def step(n, carry):
        m, r = lax.div(n, held // rows), lax.rem(n, held // rows)
        row = lax.broadcasted_iota(jnp.int32, (rows, cells), 0) + n * rows
        value = jnp.where(places[0] == row, weights[0], 0.0)
        for k in range(1, 4):
            value = value + jnp.where(places[k] == row, weights[k], 0.0)
        sampling[m, pl.ds(pl.multiple_of(r * rows, rows), rows), :] = value.astype(BF16)
        return carry

    lax.fori_loop(0, blocks * held // rows, step, 0)


def resample_kernel(*refs, chosen):
    samplings, held, out = refs[:2], refs[2:-1], refs[-1]
    core = lax.rem(lax.axis_index("ch"), 2)
    for c in range(2):

        @pl.when(core == c)
        def _(sampling=samplings[chosen ^ c]):
            total = jnp.zeros(out.shape, F32)
            for m, block in enumerate(held):
                total = total + jnp.dot(block[...], sampling[m], preferred_element_type=F32)
            out[...] = total.astype(BF16)


def add_kernel(a, b, out):
    out[...] = (a[...].astype(F32) + b[...].astype(F32)).astype(BF16)


def choose_kernel(a, b, out):
    out[...] = jnp.where(lax.rem(lax.axis_index("ch"), 2) == 0, a[...], b[...])


def expand_kernel(wa, wb, wc, wd, bias, *refs):
    pieces, out = [ref[...].astype(F32) for ref in refs[:-1]], refs[-1]
    first = lax.rem(lax.axis_index("ch"), 2) == 0
    near, far = [
        jnp.where(
            first,
            jnp.concatenate([a[...], b[...]], axis=0),
            jnp.concatenate([b[...], a[...]], axis=0),
        )
        for a, b in ((wa, wb), (wc, wd))
    ]
    sums = [pieces[0] + pieces[1], pieces[2] + pieces[3]]
    sums = [value.astype(BF16) for value in sums]
    z = lax.dot_general(
        jnp.concatenate([near, far], axis=0),
        jnp.concatenate(sums, axis=0),
        (((0,), (0,)), ((), ())),
        preferred_element_type=F32,
    )
    out[...] = (z + bias[...]).astype(BF16)


def sampled_by_request(mine, other, core, request_cell, corner_slot, corner_frac, n_az):
    share = mine.shape[0] // 2
    halves = jnp.where(core == 0, jnp.stack([mine, other]), jnp.stack([other, mine]))
    hidden = lax.dynamic_slice_in_dim(halves, core * share, share, 1)
    hidden = hidden.transpose(1, 0, 2).reshape(share, -1)
    asked = lax.all_to_all(request_cell, "az", split_axis=0, concat_axis=0, tiled=True)
    picked = jnp.take(hidden, asked, axis=1)
    arrived = lax.all_to_all(picked, "az", split_axis=1, concat_axis=1, tiled=True)
    u, v = corner_frac[0][None, :], corner_frac[1][None, :]
    weights = ((1.0 - u) * (1.0 - v), u * (1.0 - v), (1.0 - u) * v, u * v)
    sampled = jnp.zeros((share, corner_slot.shape[1]), F32)
    for k in range(4):
        sampled = sampled + weights[k] * jnp.take(arrived, corner_slot[k], axis=1).astype(F32)
    sampled = sampled.astype(BF16)
    zeros = jnp.zeros_like(sampled)
    placed = jnp.where(core == 0, jnp.stack([sampled, zeros]), jnp.stack([zeros, sampled]))
    return placed.reshape(2 * share, -1)


def local(
    features,
    conv1_weight,
    conv1_bias,
    conv2_weight,
    conv2_bias,
    request_cell,
    corner_slot,
    corner_frac,
    expand_weight,
    expand_bias,
):
    n_az, n_ch = lax.axis_size("az"), lax.axis_size("ch")
    az, ch = lax.axis_index("az"), lax.axis_index("ch")
    core = lax.rem(ch, 2)
    inputs, columns, length = features.shape
    share = conv1_weight.shape[0]
    total = share * n_ch
    cells = corner_slot.shape[1]
    slots = request_cell.shape[0]
    direct = n_az == TILES
    half = columns // 2

    def swap(x, mask):
        return lax.ppermute(x, "ch", [(i, i ^ mask) for i in range(n_ch)])

    def joint(x, target):
        pairs = []
        for a in range(n_az):
            for c in range(n_ch):
                pairs.append((a * n_ch + c, target(a, c % 2) * n_ch + c))
        return lax.ppermute(x, ("az", "ch"), pairs)

    w1 = conv1_weight.transpose(1, 2, 0, 3)
    w2 = conv2_weight.transpose(1, 2, 0, 3)
    w1_y = swap(w1, 2)
    own = lax.optimization_barrier(features.reshape(inputs, columns * length))
    (edge,) = call(edge_kernel, [shape((inputs, half * length), BF16)], own, flops=4 * 10**9)
    halo = joint(edge, lambda a, k: (a + 1 - 2 * k) % n_az)
    edge, w1_again, w2_again, conv1_bias, conv2_bias = lax.optimization_barrier(
        (edge, w1, w2, conv1_bias, conv2_bias)
    )

    bias = jnp.concatenate([conv1_bias, conv2_bias]).reshape(1, 2 * share)
    bias_y = swap(bias, 2)
    if direct:
        (table,) = call(
            functools.partial(table_kernel, sectors=n_az, columns=columns),
            [shape((8, cells), F32)],
            request_cell.reshape(-1, length),
            corner_slot,
            corner_frac,
            touched=0,
        )
        w1_y, table = lax.optimization_barrier((w1_y, table))
    own_rows, own_stack, own_inner = call(
        own_rows_kernel,
        [
            shape((columns * inputs, length), BF16),
            shape((3 * share, 3 * inputs), BF16),
            shape((columns - 2, share, length), F32),
        ],
        own,
        w1,
        touched=0,
    )
    w1_y, bias_y, own_inner = lax.optimization_barrier((w1_y, bias_y, own_inner))
    bias = jnp.concatenate([bias, bias_y])
    bias_core = swap(bias, 1)

    w1_far = swap(w1_y, 1)
    w1_core = swap(w1_again, 1)
    w2_core = swap(w2_again, 1)
    w1_near, w2_plane, inner = call(
        prepare_kernel,
        [
            shape((3 * 2 * share, 3 * inputs), BF16),
            shape((3 * 2 * share, 3 * total), BF16),
            shape((columns - 2, 2 * share, length), F32),
        ],
        own_rows,
        own_stack,
        own_inner,
        w1_core,
        w2,
        w2_core,
        scratch=[pltpu.VMEM((3 * share, 3 * inputs), BF16)],
    )
    (halo,) = call(rows_kernel, [shape((half * inputs, length), BF16)], halo, flops=10**10)
    (mine,) = call(
        conv_kernel,
        [shape((2 * share, half * length), BF16)],
        own,
        halo,
        w1_near,
        w2_plane,
        inner,
        w1_y,
        w1_far,
        bias,
        bias_core,
        scratch=[
            pltpu.VMEM(((columns + half) * inputs, length), BF16),
            pltpu.VMEM((3 * 2 * share, 3 * inputs), BF16),
            pltpu.VMEM((columns * total, length), BF16),
            pltpu.VMEM((2, total, 1), F32),
        ],
        flops=2 * 9 * inputs * total * columns * length,
    )
    outs = expand_weight.shape[1] // n_ch

    def expansion_slices(expand_weight):
        slices = [
            lax.dynamic_slice_in_dim(expand_weight, (ch ^ f) * outs, outs, 1) for f in range(n_ch)
        ]
        slices[1], slices[3] = swap(slices[1], 1), swap(slices[3], 3)
        slices[1], slices[2] = lax.optimization_barrier((slices[1], slices[2]))
        slices[2] = swap(slices[2], 2)
        return slices

    if direct:
        turns = TILES // 2
        mine, table = lax.optimization_barrier((mine, table))
        partner_table = joint(table, lambda a, k: a ^ 1)
        held = [mine]
        for m in range(1, turns):
            held.append(joint(mine, lambda a, k, m=m: (a + 2 * m) % n_az))
        expand_weight, partner_table = lax.optimization_barrier((expand_weight, partner_table))
        samplings = []
        for entries in (table, partner_table):
            (sampling,) = call(
                sampling_kernel,
                [shape((turns, half * length, cells), BF16)],
                entries,
                touched=0,
            )
            samplings.append(sampling)
        slices = expansion_slices(expand_weight)
        held[0], slices = lax.optimization_barrier((held[0], slices))
        tile = shape((2 * share, cells), BF16)
        sent, kept = [
            call(
                functools.partial(resample_kernel, chosen=chosen),
                [tile],
                *samplings,
                *held,
                flops=2 * share * slots * cells,
            )[0]
            for chosen in (1, 0)
        ]
        (kept,) = call(add_kernel, [tile], kept, swap(sent, 1))
        other_plane, same_plane = [], []
        for a in range(n_az):
            for c in range(n_ch):
                other_plane.append((a * n_ch + c, (a ^ (c % 2)) * n_ch + (c ^ 2)))
                if c % 2:
                    same_plane.append((a * n_ch + c, (a ^ 1) * n_ch + c))
        far = lax.ppermute(kept, ("az", "ch"), other_plane)
        near = lax.ppermute(kept, ("az", "ch"), same_plane)
        far, near = lax.optimization_barrier((far, near))
        (near,) = call(choose_kernel, [tile], kept, near)
    else:
        near = sampled_by_request(
            mine, swap(mine, 1), core, request_cell, corner_slot, corner_frac, n_az
        )
        far = swap(near, 2)
        slices = expansion_slices(expand_weight)
    pieces = [near, swap(near, 1), far, swap(far, 1)]
    (out,) = call(
        expand_kernel,
        [shape((outs, cells), BF16)],
        *slices,
        expand_bias.reshape(outs, 1),
        *pieces,
        flops=4 * outs * total * cells,
    )
    return out


def solution(mesh):
    return jax.shard_map(
        local,
        mesh=mesh,
        in_specs=(
            P(None, "az", None),
            P("ch", None, None, None),
            P("ch"),
            P("ch", None, None, None),
            P("ch"),
            P("az"),
            P(None, "az"),
            P(None, "az"),
            P("ch", None),
            P("ch"),
        ),
        out_specs=P("ch", "az"),
        check_vma=False,
    )
```

```python
import functools

import jax
import jax.numpy as jnp
from jax import lax
from jax.experimental import pallas as pl
from jax.experimental.pallas import tpu as pltpu
from jax.sharding import PartitionSpec as P

BF16 = jnp.bfloat16
F32 = jnp.float32
VMEM_LIMIT = 20 * 1024 * 1024
TILES = 8


def call(kernel, outs, *args, scratch=(), flops=0, touched=None):
    vmem = pl.BlockSpec(memory_space=pltpu.VMEM)
    if touched is None:
        touched = sum(a.size * a.dtype.itemsize for a in args)
        touched += sum(o.size * o.dtype.itemsize for o in outs)
    return pl.pallas_call(
        kernel,
        out_shape=tuple(outs),
        in_specs=[vmem] * len(args),
        out_specs=tuple(vmem for _ in outs),
        scratch_shapes=list(scratch),
        compiler_params=pltpu.CompilerParams(vmem_limit_bytes=VMEM_LIMIT),
        cost_estimate=pl.CostEstimate(flops=flops, bytes_accessed=touched, transcendentals=0),
    )(*args)


def shape(dims, dtype):
    return jax.ShapeDtypeStruct(dims, dtype)


def range_sum(z, rows):
    length = z.shape[1]
    lane = lax.broadcasted_iota(jnp.int32, (rows, length), 1)
    before = jnp.where(lane == 0, 0.0, pltpu.roll(z[:rows], 1, 1))
    after = jnp.where(lane == length - 1, 0.0, pltpu.roll(z[2 * rows :], length - 1, 1))
    return z[rows : 2 * rows] + before + after


def stack_weights(dest, pieces, places, inputs):
    rows = dest.shape[0] // 3
    share = pieces[0].shape[2]
    for piece, place in zip(pieces, places):
        for i in range(3):
            for j in range(3):
                dest[pl.ds(j * rows + place, share), i * inputs : (i + 1) * inputs] = piece[i, j]


def edge_kernel(own, edge):
    width = edge.shape[1]
    at = pl.multiple_of((1 - lax.rem(lax.axis_index("ch"), 2)) * width, width)
    edge[...] = own[:, pl.ds(at, width)]


def rows_kernel(wide, rows):
    channels, length = wide.shape[0], rows.shape[1]
    for a in range(rows.shape[0] // channels):
        rows[a * channels : (a + 1) * channels, :] = wide[:, a * length : (a + 1) * length]


def own_rows_kernel(own, weight, xs, stack, inner):
    share, inputs, length = weight.shape[2], weight.shape[3], xs.shape[1]
    for i in range(3):
        for j in range(3):
            stack[j * share : (j + 1) * share, i * inputs : (i + 1) * inputs] = weight[i, j]
    for a in range(own.shape[1] // length):
        xs[a * inputs : (a + 1) * inputs, :] = own[:, a * length : (a + 1) * length]
    for n in range(inner.shape[0]):
        z = jnp.dot(stack[...], xs[n * inputs : (n + 3) * inputs, :], preferred_element_type=F32)
        inner[n] = range_sum(z, share)


def prepare_kernel(xs, own_stack, own_inner, w1b, w2a, w2b, near, plane, inner, stack):
    core = lax.rem(lax.axis_index("ch"), 2)
    share, inputs = w1b.shape[2], w1b.shape[3]
    places = [pl.multiple_of((core ^ f) * share, share) for f in range(2)]
    stack_weights(plane, (w2a, w2b), places, w2a.shape[3])
    for i in range(3):
        for j in range(3):
            stack[j * share : (j + 1) * share, i * inputs : (i + 1) * inputs] = w1b[i, j]
    for j in range(3):
        rows = slice(j * share, (j + 1) * share)
        for source, place in zip((own_stack, stack), places):
            near[pl.ds(2 * j * share + place, share), :] = source[rows, :]
    for n in range(inner.shape[0]):
        z = jnp.dot(stack[...], xs[n * inputs : (n + 3) * inputs, :], preferred_element_type=F32)
        inner[n, pl.ds(places[0], share), :] = own_inner[n]
        inner[n, pl.ds(places[1], share), :] = range_sum(z, share)


def conv_kernel(
    own, halo, near, w2s, inner, w1c, w1d, bias, bias_core, out, xs, far, hs, bs
):
    inputs, length = own.shape[0], xs.shape[1]
    ch = lax.axis_index("ch")
    core = lax.rem(ch, 2)
    columns = own.shape[1] // length
    extra = halo.shape[0] // inputs
    share = w1c.shape[2]
    total = bs.shape[1]
    for a in range(columns):
        at = pl.multiple_of((a + extra * (1 - core)) * inputs, inputs)
        xs[pl.ds(at, inputs), :] = own[:, a * length : (a + 1) * length]
    for a in range(extra):
        at = pl.multiple_of((a + columns * core) * inputs, inputs)
        xs[pl.ds(at, inputs), :] = halo[a * inputs : (a + 1) * inputs, :]
    stack_weights(
        far, (w1c, w1d), [pl.multiple_of((core ^ f) * share, share) for f in range(2)], inputs
    )
    lane = lax.broadcasted_iota(jnp.int32, (share, 2 * share), 1)
    sub = lax.broadcasted_iota(jnp.int32, (share, 2 * share), 0)
    rows = (bias[0:1, :], bias_core[0:1, :], bias[1:2, :], bias_core[1:2, :])
    for f, row in enumerate(rows):
        at = pl.multiple_of((ch ^ f) * share, share)
        for n in range(2):
            column = jnp.sum(jnp.where(lane == sub + n * share, row, 0.0), axis=1, keepdims=True)
            bs[n, pl.ds(at, share), :] = column
    wide = 2 * share
    near_at = pl.multiple_of((ch - core) * share, wide)
    far_at = pl.multiple_of(total - wide - near_at, wide)
    bias2 = bs[1, pl.ds(near_at, wide), :]
    hidden_columns = hs.shape[0] // total

    def keep(h, at, value):
        value = jnp.maximum(value + bs[0, pl.ds(at, wide), :], 0.0)
        hs[pl.ds(pl.multiple_of(h * total + at, wide), wide), :] = value.astype(BF16)

    inners = inner.shape[0]
    for n in range(hidden_columns - inners):
        h = n + inners * core
        rows = pl.ds(pl.multiple_of(h * inputs, inputs), 3 * inputs)
        z = jnp.dot(near[...], xs[rows, :], preferred_element_type=F32)
        keep(h, near_at, range_sum(z, wide))
    for n in range(inners):
        keep(n + inners * (1 - core), near_at, inner[n])
    for h in range(hidden_columns):
        z = jnp.dot(far[...], xs[h * inputs : (h + 3) * inputs, :], preferred_element_type=F32)
        keep(h, far_at, range_sum(z, wide))
    for g in range(hidden_columns - 2):
        z = jnp.dot(w2s[...], hs[g * total : (g + 3) * total, :], preferred_element_type=F32)
        value = jnp.maximum(range_sum(z, wide) + bias2, 0.0)
        out[:, g * length : (g + 1) * length] = value.astype(BF16)


def table_kernel(asks, slot, frac, table, *, sectors, columns):
    blocks, length = asks.shape
    width = blocks * length // sectors
    lhs = jnp.concatenate(
        [lax.rem(asks[...], length).astype(F32), lax.div(asks[...], length).astype(F32)], axis=0
    ).astype(BF16)
    cells = slot.shape[1]
    high = lax.broadcasted_iota(jnp.int32, (blocks, cells), 0)
    low = lax.broadcasted_iota(jnp.int32, (length, cells), 0)
    for k in range(4):
        q = slot[k : k + 1, :]
        hot = jnp.where(low == lax.rem(q, length), 1.0, 0.0).astype(BF16)
        z = jnp.dot(lhs, hot, preferred_element_type=F32)
        mask = high == lax.div(q, length)
        at = jnp.sum(jnp.where(mask, z[:blocks], 0.0), axis=0, keepdims=True)
        column = jnp.sum(jnp.where(mask, z[blocks:], 0.0), axis=0, keepdims=True)
        sector = lax.div(q, width).astype(F32)
        table[k : k + 1, :] = (sector * columns + column) * length + at
    u, v = frac[0:1, :], frac[1:2, :]
    weights = ((1.0 - u) * (1.0 - v), u * (1.0 - v), (1.0 - u) * v, u * v)
    for k in range(4):
        table[4 + k : 5 + k, :] = weights[k]


def sampling_kernel(table, sampling):
    az, core = lax.axis_index("az"), lax.rem(lax.axis_index("ch"), 2)
    blocks, held, cells = sampling.shape
    z, x = lax.div(az, 2), lax.rem(az, 2)
    rows = 32
    places, weights = [], []
    for k in range(4):
        at = table[k : k + 1, :].astype(jnp.int32)
        sector, cell = lax.div(at, 2 * held), lax.rem(at, 2 * held)
        block = lax.rem(z - lax.div(sector, 2) + blocks, blocks)
        used = (lax.rem(sector, 2) == x) & (lax.div(cell, held) == core)
        places.append(jnp.where(used, block * held + lax.rem(cell, held), -1))
        weights.append(table[4 + k : 5 + k, :])

    def step(n, carry):
        m, r = lax.div(n, held // rows), lax.rem(n, held // rows)
        row = lax.broadcasted_iota(jnp.int32, (rows, cells), 0) + n * rows
        value = jnp.where(places[0] == row, weights[0], 0.0)
        for k in range(1, 4):
            value = value + jnp.where(places[k] == row, weights[k], 0.0)
        sampling[m, pl.ds(pl.multiple_of(r * rows, rows), rows), :] = value.astype(BF16)
        return carry

    lax.fori_loop(0, blocks * held // rows, step, 0)


def resample_kernel(*refs, chosen):
    samplings, held, out = refs[:2], refs[2:-1], refs[-1]
    core = lax.rem(lax.axis_index("ch"), 2)
    for c in range(2):

        @pl.when(core == c)
        def _(sampling=samplings[chosen ^ c]):
            total = jnp.zeros(out.shape, F32)
            for m, block in enumerate(held):
                total = total + jnp.dot(block[...], sampling[m], preferred_element_type=F32)
            out[...] = total.astype(BF16)


def add_kernel(a, b, out):
    out[...] = (a[...].astype(F32) + b[...].astype(F32)).astype(BF16)


def choose_kernel(a, b, out):
    out[...] = jnp.where(lax.rem(lax.axis_index("ch"), 2) == 0, a[...], b[...])


def expand_kernel(wa, wb, wc, wd, bias, *refs):
    pieces, out = [ref[...].astype(F32) for ref in refs[:-1]], refs[-1]
    first = lax.rem(lax.axis_index("ch"), 2) == 0
    near, far = [
        jnp.where(
            first,
            jnp.concatenate([a[...], b[...]], axis=0),
            jnp.concatenate([b[...], a[...]], axis=0),
        )
        for a, b in ((wa, wb), (wc, wd))
    ]
    sums = [pieces[0] + pieces[1], pieces[2] + pieces[3]]
    sums = [value.astype(BF16) for value in sums]
    z = lax.dot_general(
        jnp.concatenate([near, far], axis=0),
        jnp.concatenate(sums, axis=0),
        (((0,), (0,)), ((), ())),
        preferred_element_type=F32,
    )
    out[...] = (z + bias[...]).astype(BF16)


def sampled_by_request(mine, other, core, request_cell, corner_slot, corner_frac, n_az):
    share = mine.shape[0] // 2
    halves = jnp.where(core == 0, jnp.stack([mine, other]), jnp.stack([other, mine]))
    hidden = lax.dynamic_slice_in_dim(halves, core * share, share, 1)
    hidden = hidden.transpose(1, 0, 2).reshape(share, -1)
    asked = lax.all_to_all(request_cell, "az", split_axis=0, concat_axis=0, tiled=True)
    picked = jnp.take(hidden, asked, axis=1)
    arrived = lax.all_to_all(picked, "az", split_axis=1, concat_axis=1, tiled=True)
    u, v = corner_frac[0][None, :], corner_frac[1][None, :]
    weights = ((1.0 - u) * (1.0 - v), u * (1.0 - v), (1.0 - u) * v, u * v)
    sampled = jnp.zeros((share, corner_slot.shape[1]), F32)
    for k in range(4):
        sampled = sampled + weights[k] * jnp.take(arrived, corner_slot[k], axis=1).astype(F32)
    sampled = sampled.astype(BF16)
    zeros = jnp.zeros_like(sampled)
    placed = jnp.where(core == 0, jnp.stack([sampled, zeros]), jnp.stack([zeros, sampled]))
    return placed.reshape(2 * share, -1)


def local(
    features,
    conv1_weight,
    conv1_bias,
    conv2_weight,
    conv2_bias,
    request_cell,
    corner_slot,
    corner_frac,
    expand_weight,
    expand_bias,
):
    n_az, n_ch = lax.axis_size("az"), lax.axis_size("ch")
    az, ch = lax.axis_index("az"), lax.axis_index("ch")
    core = lax.rem(ch, 2)
    inputs, columns, length = features.shape
    share = conv1_weight.shape[0]
    total = share * n_ch
    cells = corner_slot.shape[1]
    slots = request_cell.shape[0]
    direct = n_az == TILES
    half = columns // 2

    def swap(x, mask):
        return lax.ppermute(x, "ch", [(i, i ^ mask) for i in range(n_ch)])

    def joint(x, target):
        pairs = []
        for a in range(n_az):
            for c in range(n_ch):
                pairs.append((a * n_ch + c, target(a, c % 2) * n_ch + c))
        return lax.ppermute(x, ("az", "ch"), pairs)

    w1 = conv1_weight.transpose(1, 2, 0, 3)
    w2 = conv2_weight.transpose(1, 2, 0, 3)
    w1_y = swap(w1, 2)
    own = lax.optimization_barrier(features.reshape(inputs, columns * length))
    (edge,) = call(edge_kernel, [shape((inputs, half * length), BF16)], own, flops=4 * 10**9)
    halo = joint(edge, lambda a, k: (a + 1 - 2 * k) % n_az)
    edge, w1_again, w2_again, conv1_bias, conv2_bias = lax.optimization_barrier(
        (edge, w1, w2, conv1_bias, conv2_bias)
    )

    bias = jnp.concatenate([conv1_bias, conv2_bias]).reshape(1, 2 * share)
    bias_y = swap(bias, 2)
    if direct:
        (table,) = call(
            functools.partial(table_kernel, sectors=n_az, columns=columns),
            [shape((8, cells), F32)],
            request_cell.reshape(-1, length),
            corner_slot,
            corner_frac,
            touched=0,
        )
        w1_y, table = lax.optimization_barrier((w1_y, table))
    own_rows, own_stack, own_inner = call(
        own_rows_kernel,
        [
            shape((columns * inputs, length), BF16),
            shape((3 * share, 3 * inputs), BF16),
            shape((columns - 2, share, length), F32),
        ],
        own,
        w1,
        touched=0,
    )
    w1_y, bias_y, own_inner = lax.optimization_barrier((w1_y, bias_y, own_inner))
    bias = jnp.concatenate([bias, bias_y])
    bias_core = swap(bias, 1)

    w1_far = swap(w1_y, 1)
    w1_core = swap(w1_again, 1)
    w2_core = swap(w2_again, 1)
    w1_near, w2_plane, inner = call(
        prepare_kernel,
        [
            shape((3 * 2 * share, 3 * inputs), BF16),
            shape((3 * 2 * share, 3 * total), BF16),
            shape((columns - 2, 2 * share, length), F32),
        ],
        own_rows,
        own_stack,
        own_inner,
        w1_core,
        w2,
        w2_core,
        scratch=[pltpu.VMEM((3 * share, 3 * inputs), BF16)],
    )
    (halo,) = call(rows_kernel, [shape((half * inputs, length), BF16)], halo, flops=10**10)
    (mine,) = call(
        conv_kernel,
        [shape((2 * share, half * length), BF16)],
        own,
        halo,
        w1_near,
        w2_plane,
        inner,
        w1_y,
        w1_far,
        bias,
        bias_core,
        scratch=[
            pltpu.VMEM(((columns + half) * inputs, length), BF16),
            pltpu.VMEM((3 * 2 * share, 3 * inputs), BF16),
            pltpu.VMEM((columns * total, length), BF16),
            pltpu.VMEM((2, total, 1), F32),
        ],
        flops=2 * 9 * inputs * total * columns * length,
    )
    outs = expand_weight.shape[1] // n_ch

    def expansion_slices(expand_weight):
        slices = [
            lax.dynamic_slice_in_dim(expand_weight, (ch ^ f) * outs, outs, 1) for f in range(n_ch)
        ]
        slices[1], slices[3] = swap(slices[1], 1), swap(slices[3], 3)
        slices[1], slices[2] = lax.optimization_barrier((slices[1], slices[2]))
        slices[2] = swap(slices[2], 2)
        return slices

    if direct:
        turns = TILES // 2
        mine, table = lax.optimization_barrier((mine, table))
        partner_table = joint(table, lambda a, k: a ^ 1)
        held = [mine]
        for m in range(1, turns):
            held.append(joint(mine, lambda a, k, m=m: (a + 2 * m) % n_az))
        expand_weight, partner_table = lax.optimization_barrier((expand_weight, partner_table))
        samplings = []
        for entries in (table, partner_table):
            (sampling,) = call(
                sampling_kernel,
                [shape((turns, half * length, cells), BF16)],
                entries,
                touched=0,
            )
            samplings.append(sampling)
        slices = expansion_slices(expand_weight)
        held[0], slices = lax.optimization_barrier((held[0], slices))
        tile = shape((2 * share, cells), BF16)
        sent, kept = [
            call(
                functools.partial(resample_kernel, chosen=chosen),
                [tile],
                *samplings,
                *held,
                flops=2 * share * slots * cells,
            )[0]
            for chosen in (1, 0)
        ]
        (kept,) = call(add_kernel, [tile], kept, swap(sent, 1))
        other_plane, same_plane = [], []
        for a in range(n_az):
            for c in range(n_ch):
                other_plane.append((a * n_ch + c, (a ^ (c % 2)) * n_ch + (c ^ 2)))
                if c % 2:
                    same_plane.append((a * n_ch + c, (a ^ 1) * n_ch + c))
        far = lax.ppermute(kept, ("az", "ch"), other_plane)
        near = lax.ppermute(kept, ("az", "ch"), same_plane)
        far, near = lax.optimization_barrier((far, near))
        (near,) = call(choose_kernel, [tile], kept, near)
    else:
        near = sampled_by_request(
            mine, swap(mine, 1), core, request_cell, corner_slot, corner_frac, n_az
        )
        far = swap(near, 2)
        slices = expansion_slices(expand_weight)
    pieces = [near, swap(near, 1), far, swap(far, 1)]
    (out,) = call(
        expand_kernel,
        [shape((outs, cells), BF16)],
        *slices,
        expand_bias.reshape(outs, 1),
        *pieces,
        flops=4 * outs * total * cells,
    )
    return out


def solution(mesh):
    return jax.shard_map(
        local,
        mesh=mesh,
        in_specs=(
            P(None, "az", None),
            P("ch", None, None, None),
            P("ch"),
            P("ch", None, None, None),
            P("ch"),
            P("az"),
            P(None, "az"),
            P(None, "az"),
            P("ch", None),
            P("ch"),
        ),
        out_specs=P("ch", "az"),
        check_vma=False,
    )
```
